512 devices in a mesh: dp: 32 (over z_hi, y, core), mp: 16 (over z_lo, x).
Axes of the slice: x: 4, y: 8, z: 8 (z_hi: 2, z_lo: 4; z = z_hi * 4 + z_lo), core: 2. Of those that a mesh axis runs over, the one named last changes fastest.
Arguments:
- tokens: bfloat16 [256, 8192], P('mp', 'dp'), may hold values from -6 to 6
- gate_weight: bfloat16 [8192, 14336], P('dp', 'mp'), may hold values from -0.0625 to 0.0625
- up_weight: bfloat16 [8192, 14336], P('dp', 'mp'), may hold values from -0.0625 to 0.0625
- down_weight: bfloat16 [14336, 8192], P('mp', 'dp'), may hold values from -0.046875 to 0.046875
- cotangent: bfloat16 [256, 8192], P('mp', 'dp'), may hold values from -6 to 6
Outputs:
- output: bfloat16 [256, 8192], P('mp', 'dp')
- tokens_grad: bfloat16 [256, 8192], P('mp', 'dp')
- gate_grad: bfloat16 [8192, 14336], P('dp', 'mp')
- up_grad: bfloat16 [8192, 14336], P('dp', 'mp')
- down_grad: bfloat16 [14336, 8192], P('mp', 'dp')
The draws below stay inside these ranges and needn't reach their ends.
All inputs are finite; a program needn't handle non-finite values.
Results may differ from the reference program's by a relative error of at most 0.0049.
Values may be sent and summed in bfloat16 or wider, within the bound.
A program may use at most 64 MiB of HBM per device.

```python
import math
import jax
import jax.numpy as jnp

D = 8192
FF = 14336
TOKENS = 256


def block_levels(stream_key, dims, pieces, least, top_value):
    def one(position, blocks):
        draws = jax.random.uniform(jax.random.fold_in(jax.random.fold_in(stream_key, 6), position), (blocks,), jnp.float32, least / len(pieces), top_value / len(pieces))
        return jnp.repeat(jnp.exp(draws), dims[position] // blocks).reshape((-1,) + (1,) * (len(dims) - position - 1))

    level = one(*pieces[0])
    for cut in pieces[1:]:
        level = level * one(*cut)
    return level


def bell_draw(stream_key, shape, spread, bound, shards=(), held_as=jnp.bfloat16):
    array = spread * jax.random.normal(stream_key, shape, jnp.float32)
    if shards:
        array = array * block_levels(stream_key, shape, shards, -0.22, 0.18)
    return jnp.clip(array, -bound, bound).astype(held_as)


def setup_inputs(seed: int = 0) -> dict:
    splits = jax.random.split(jax.random.key(seed), 6)
    return {
        "tokens": bell_draw(splits[0], (TOKENS, D), 1.0, 6.0, ((0, 16), (1, 32))),
        "gate_weight": bell_draw(splits[1], (D, FF), D ** -0.5, 0.0625, ((0, 32), (1, 16))),
        "up_weight": bell_draw(splits[2], (D, FF), D ** -0.5, 0.0625, ((0, 32), (1, 16))),
        "down_weight": bell_draw(splits[3], (FF, D), FF ** -0.5, 0.046875, ((0, 16), (1, 32))),
        "cotangent": bell_draw(splits[4], (TOKENS, D), 1.0, 6.0, ((0, 16), (1, 32))),
    }


def reference(tokens, gate_weight, up_weight, down_weight, cotangent):
    gate_sum = jnp.dot(tokens, gate_weight, preferred_element_type=jnp.float32)
    up_sum = jnp.dot(tokens, up_weight, preferred_element_type=jnp.float32)
    sigmoid_gate = jax.nn.sigmoid(gate_sum)
    hidden = (gate_sum * sigmoid_gate * up_sum).astype(jnp.bfloat16)
    output = jnp.dot(hidden, down_weight, preferred_element_type=jnp.float32).astype(jnp.bfloat16)
    grad_hidden = jnp.dot(cotangent, down_weight.T, preferred_element_type=jnp.float32)
    grad_gate = (grad_hidden * up_sum * sigmoid_gate * (1.0 + gate_sum * (1.0 - sigmoid_gate))).astype(jnp.bfloat16)
    grad_up = (grad_hidden * gate_sum * sigmoid_gate).astype(jnp.bfloat16)
    tokens_grad = (jnp.dot(grad_gate, gate_weight.T, preferred_element_type=jnp.float32) + jnp.dot(grad_up, up_weight.T, preferred_element_type=jnp.float32)).astype(jnp.bfloat16)
    factor = 1.0 / math.sqrt(tokens.shape[0])
    gate_grad = (jnp.dot(tokens.T, grad_gate, preferred_element_type=jnp.float32) * factor).astype(jnp.bfloat16)
    up_grad = (jnp.dot(tokens.T, grad_up, preferred_element_type=jnp.float32) * factor).astype(jnp.bfloat16)
    down_grad = (jnp.dot(hidden.T, cotangent, preferred_element_type=jnp.float32) * factor).astype(jnp.bfloat16)
    return (output, tokens_grad, gate_grad, up_grad, down_grad)
```

```python
import math

import jax
import jax.numpy as jnp
from jax import lax
from jax.experimental import pallas as pl
from jax.experimental.pallas import tpu as pltpu
from jax.sharding import PartitionSpec as P

MESH = pl.DeviceIdType.MESH
F32 = jnp.float32
BF16 = jnp.bfloat16
RING = 8
ROWS = 16
CODE_SCALE = float(2**18)


def encode(x):
    x = x * CODE_SCALE
    return (x * x * (x * jnp.abs(x))).astype(BF16)


def decode(code):
    y = code.astype(F32)
    root = lax.rsqrt(lax.rsqrt(jnp.abs(y))) * (1.0 / CODE_SCALE)
    return jnp.where(y < 0, -root, root)


def dot(left, right):
    return jnp.dot(left, right, preferred_element_type=F32)


def dot_last(left, right):
    return lax.dot_general(left, right, (((1,), (1,)), ((), ())), preferred_element_type=F32)


def dot_first(left, right):
    return lax.dot_general(left, right, (((0,), (0,)), ((), ())), preferred_element_type=F32)


def kernel(
    tok_ref, cot_ref, wg_hbm, wu_hbm, wd_hbm,
    out_ref, tgrad_ref, ggrad_ref, ugrad_ref, dgrad_ref,
    wg, wu, wd, sg, su, sd,
    tg, cg, ts, cs, acc,
    sendp, recvp, sendm, recvm, sendz, recvz,
    hgu, part, parts,
    load_sem, wsib_ss, wsib_rs, gat_ss, gat_rs, fwd_ss, fwd_rs,
    rp_ss, rp_rs, rm_ss, rm_rs, z_ss, z_rs,
    ap_ss, ap_rs, am_ss, am_rs, af_ss, af_rs, o_ss, o_rs,
):
    dp, mp = lax.axis_index("dp"), lax.axis_index("mp")
    core, y, zh = dp % 2, (dp // 2) % RING, dp // 16
    sib = (dp + 1 - 2 * core, mp)
    yplus = (zh * 16 + ((y + 1) % RING) * 2 + core, mp)
    yminus = (zh * 16 + ((y + RING - 1) % RING) * 2 + core, mp)
    zother = ((1 - zh) * 16 + y * 2 + core, mp)
    n_mp = 16
    factor = 1.0 / math.sqrt(ROWS * n_mp)

    def remote(src, dst, ss, rs, to):
        return pltpu.make_async_remote_copy(
            src_ref=src, dst_ref=dst, send_sem=ss, recv_sem=rs,
            device_id=to, device_id_type=MESH,
        )

    def rows16(index):
        return pl.ds(pl.multiple_of(index * ROWS, ROWS), ROWS)

    loads = [
        pltpu.make_async_copy(src, dst, load_sem.at[i])
        for i, (src, dst) in enumerate(((wg_hbm, wg), (wu_hbm, wu), (wd_hbm, wd)))
    ]
    for copy in loads:
        copy.start()

    barrier = pltpu.get_barrier_semaphore()
    for to in (sib, yplus, yminus, zother):
        pl.semaphore_signal(barrier, inc=1, device_id=to, device_id_type=MESH)
    for k in range(1, n_mp):
        pl.semaphore_signal(barrier, inc=1, device_id=(dp, (mp + k) % n_mp), device_id_type=MESH)
    pl.semaphore_wait(barrier, 4 + n_mp - 1)

    gathers = []
    for i, (src, dst) in enumerate(((tok_ref, tg), (cot_ref, cg))):
        group = []
        for k in range(1, n_mp):
            copy = remote(
                src, dst.at[rows16(mp)], gat_ss.at[i, k], gat_rs.at[i, k], (dp, (mp + k) % n_mp)
            )
            copy.start()
            group.append(copy)
        gathers.append(group)
    wsib = [
        remote(src, dst, wsib_ss.at[i], wsib_rs.at[i], sib)
        for i, (src, dst) in enumerate(((wg_hbm, sg), (wu_hbm, su), (wd_hbm, sd)))
    ]
    for copy in wsib:
        copy.start()
    tg[rows16(mp), :] = tok_ref[...]
    cg[rows16(mp), :] = cot_ref[...]

    mine = pl.ds(pl.multiple_of(core * 128, 128), 128)
    theirs = pl.ds(pl.multiple_of((1 - core) * 128, 128), 128)

    def block(array, index):
        return acc[array, rows16(index), :]

    ring_p = [[None] * 3 for _ in range(4)]
    ring_m = [[None] * 3 for _ in range(3)]

    def send_p(step, array, value):
        sendp[step, array] = encode(value)
        ring_p[step][array] = remote(
            sendp.at[step, array], recvp.at[step, array],
            rp_ss.at[step, array], rp_rs.at[step, array], yplus,
        )
        ring_p[step][array].start()

    def send_m(step, array, value):
        sendm[step, array] = encode(value)
        ring_m[step][array] = remote(
            sendm.at[step, array], recvm.at[step, array],
            rm_ss.at[step, array], rm_rs.at[step, array], yminus,
        )
        ring_m[step][array].start()

    def first_hop(array):
        send_p(0, array, block(array, (y + 4) % RING))
        send_m(0, array, block(array, (y + 5) % RING))

    forwards = []
    for i, (full, half) in enumerate(((tg, ts), (cg, cs))):
        for copy in gathers[i]:
            copy.wait_recv()
        forward = remote(full.at[theirs], half, fwd_ss.at[i], fwd_rs.at[i], sib)
        forward.start()
        forwards.append(forward)
        if i == 0:
            loads[0].wait()
            loads[1].wait()
            wsib[0].wait_recv()
            wsib[1].wait_recv()
            forward.wait_recv()
            acc[0] = dot(tg[mine, :], wg[...]) + dot(ts[...], sg[...])
            first_hop(0)
            acc[1] = dot(tg[mine, :], wu[...]) + dot(ts[...], su[...])
            first_hop(1)
        else:
            loads[2].wait()
            wsib[2].wait_recv()
            forward.wait_recv()
            acc[2] = dot_last(cg[mine, :], wd[...]) + dot_last(cs[...], sd[...])
            first_hop(2)

    for step in range(3):
        for array in range(3):
            ring_p[step][array].wait_recv()
            send_p(
                step + 1, array,
                block(array, (y + 3 - step) % RING) + decode(recvp[step, array]),
            )
            ring_m[step][array].wait_recv()
            if step < 2:
                send_m(
                    step + 1, array,
                    block(array, (y + 6 + step) % RING) + decode(recvm[step, array]),
                )
            else:
                acc[array, rows16(y), :] += decode(recvm[2, array])
    swaps = []
    for array in range(3):
        ring_p[3][array].wait_recv()
        value = block(array, y) + decode(recvp[3, array])
        acc[array, rows16(y), :] = value
        sendz[array] = encode(value)
        swap = remote(sendz.at[array], recvz.at[array], z_ss.at[array], z_rs.at[array], zother)
        swap.start()
        swaps.append(swap)
    for swap in swaps:
        swap.wait_recv()
    gate = block(0, y) + decode(recvz[0])
    up = block(1, y) + decode(recvz[1])
    grad_hidden = block(2, y) + decode(recvz[2])
    sig = jax.nn.sigmoid(gate)
    own = core * RING + y
    hgu[own, 0] = (gate * sig * up).astype(BF16)
    hgu[own, 1] = (grad_hidden * up * sig * (1.0 + gate * (1.0 - sig))).astype(BF16)
    hgu[own, 2] = (grad_hidden * gate * sig).astype(BF16)

    started = []

    def pass_on(index, ss, rs, to):
        copy = remote(hgu.at[index], hgu.at[index], ss, rs, to)
        copy.start()
        started.append(copy)
        return copy

    to_sib = []
    copy_p = pass_on(own, ap_ss.at[0], ap_rs.at[0], yplus)
    copy_m = pass_on(own, am_ss.at[0], am_rs.at[0], yminus)
    to_sib.append(pass_on(own, af_ss.at[0], af_rs.at[0], sib))
    for step in range(4):
        index = core * RING + (y + 7 - step) % RING
        copy_p.wait_recv()
        if step < 3:
            copy_p = pass_on(index, ap_ss.at[step + 1], ap_rs.at[step + 1], yplus)
        to_sib.append(pass_on(index, af_ss.at[1 + step], af_rs.at[1 + step], sib))
        if step < 3:
            index = core * RING + (y + 1 + step) % RING
            copy_m.wait_recv()
            if step < 2:
                copy_m = pass_on(index, am_ss.at[step + 1], am_rs.at[step + 1], yminus)
            to_sib.append(pass_on(index, af_ss.at[5 + step], af_rs.at[5 + step], sib))
    for copy in to_sib:
        copy.wait_recv()

    hidden = hgu[:, 0].reshape(256, -1)
    grad_gate = hgu[:, 1].reshape(256, -1)
    grad_up = hgu[:, 2].reshape(256, -1)
    total_out = dot(hidden, wd[...])
    total_tg = dot_last(grad_gate, wg[...]) + dot_last(grad_up, wu[...])
    part[:, 0] = total_out.astype(BF16).reshape(n_mp, ROWS, 256)
    part[:, 1] = total_tg.astype(BF16).reshape(n_mp, ROWS, 256)
    finals = []
    for k in range(1, n_mp):
        to = (mp + k) % n_mp
        copy = remote(part.at[to], parts.at[k], o_ss.at[k], o_rs.at[k], (dp, to))
        copy.start()
        finals.append(copy)

    ggrad_ref[...] = (dot_first(tg[...], grad_gate) * factor).astype(BF16)
    ugrad_ref[...] = (dot_first(tg[...], grad_up) * factor).astype(BF16)
    dgrad_ref[...] = (dot_first(hidden, cg[...]) * factor).astype(BF16)

    sum_out = part[mp, 0].astype(F32)
    sum_tg = part[mp, 1].astype(F32)
    for k in range(1, n_mp):
        finals[k - 1].wait_recv()
        sum_out += parts[k, 0].astype(F32)
        sum_tg += parts[k, 1].astype(F32)
    out_ref[...] = sum_out.astype(BF16)
    tgrad_ref[...] = sum_tg.astype(BF16)

    for copy in gathers[0] + gathers[1] + wsib + forwards + swaps + started + finals:
        copy.wait_send()
    for hops in ring_p + ring_m:
        for copy in hops:
            copy.wait_send()


def on_device(tokens, gate_weight, up_weight, down_weight, cotangent):
    rows, width = tokens.shape
    units = gate_weight.shape[1]
    vmem = pl.BlockSpec(memory_space=pltpu.VMEM)
    hbm = pl.BlockSpec(memory_space=pl.ANY)
    dma = pltpu.SemaphoreType.DMA
    wide = pltpu.VMEM((width, units), BF16)
    tall = pltpu.VMEM((units, width), BF16)
    return pl.pallas_call(
        kernel,
        out_shape=(
            jax.ShapeDtypeStruct((rows, width), BF16),
            jax.ShapeDtypeStruct((rows, width), BF16),
            jax.ShapeDtypeStruct((width, units), BF16),
            jax.ShapeDtypeStruct((width, units), BF16),
            jax.ShapeDtypeStruct((units, width), BF16),
        ),
        in_specs=[vmem, vmem, hbm, hbm, hbm],
        out_specs=[vmem] * 5,
        scratch_shapes=[
            wide, wide, tall, wide, wide, tall,
            pltpu.VMEM((256, width), BF16), pltpu.VMEM((256, width), BF16),
            pltpu.VMEM((128, width), BF16), pltpu.VMEM((128, width), BF16),
            pltpu.VMEM((3, 128, units), F32),
            pltpu.VMEM((4, 3, ROWS, units), BF16), pltpu.VMEM((4, 3, ROWS, units), BF16),
            pltpu.VMEM((3, 3, ROWS, units), BF16), pltpu.VMEM((3, 3, ROWS, units), BF16),
            pltpu.VMEM((3, ROWS, units), BF16), pltpu.VMEM((3, ROWS, units), BF16),
            pltpu.VMEM((16, 3, ROWS, units), BF16),
            pltpu.VMEM((16, 2, ROWS, width), BF16), pltpu.VMEM((16, 2, ROWS, width), BF16),
            dma((3,)), dma((3,)), dma((3,)), dma((2, 16)), dma((2, 16)), dma((2,)), dma((2,)),
            dma((4, 3)), dma((4, 3)), dma((3, 3)), dma((3, 3)), dma((3,)), dma((3,)),
            dma((4,)), dma((4,)), dma((3,)), dma((3,)), dma((8,)), dma((8,)),
            dma((16,)), dma((16,)),
        ],
        compiler_params=pltpu.CompilerParams(
            collective_id=0, has_side_effects=True, vmem_limit_bytes=40 * 2**20
        ),
    )(tokens, cotangent, gate_weight, up_weight, down_weight)


def solution(mesh):
    in_specs = (P("mp", "dp"), P("dp", "mp"), P("dp", "mp"), P("mp", "dp"), P("mp", "dp"))
    out_specs = (P("mp", "dp"), P("mp", "dp"), P("dp", "mp"), P("dp", "mp"), P("mp", "dp"))
    return jax.shard_map(
        on_device, mesh=mesh, in_specs=in_specs, out_specs=out_specs, check_vma=False
    )
```

```python
import math

import jax
import jax.numpy as jnp
from jax import lax
from jax.experimental import pallas as pl
from jax.experimental.pallas import tpu as pltpu
from jax.sharding import PartitionSpec as P

MESH = pl.DeviceIdType.MESH
F32 = jnp.float32
BF16 = jnp.bfloat16
RING = 8
ROWS = 16
HALF = RING * ROWS
N_MP = 16
VMEM_LIMIT = 62 * 2**20
CODE_SCALE = float(2**18)


def encode(x):
    x = x * CODE_SCALE
    return (x * x * (x * jnp.abs(x))).astype(BF16)


def decode(code):
    y = code.astype(F32)
    root = lax.rsqrt(lax.rsqrt(jnp.abs(y))) * (1.0 / CODE_SCALE)
    return jnp.where(y < 0, -root, root)


def dot(left, right):
    return jnp.dot(left, right, preferred_element_type=F32)


def dot_last(left, right):
    return lax.dot_general(left, right, (((1,), (1,)), ((), ())), preferred_element_type=F32)


def dot_first(left, right):
    return lax.dot_general(left, right, (((0,), (0,)), ((), ())), preferred_element_type=F32)


def kernel(
    tok_hbm, cot_hbm, wg_hbm, wu_hbm, wd_hbm,
    out_hbm, tgrad_hbm, ggrad_hbm, ugrad_hbm, dgrad_hbm,
    wg, wu, wd, sg, su, sd,
    mine, rows, other, full, acc, send, recv, sendz, recvz,
    hid, gug, part, parts, small, ggrad, ugrad, dgrad,
    load_sem, mine_sem, wsib_ss, wsib_rs, gat_ss, gat_rs, oth_ss, oth_rs,
    rs_ss, rs_rs, z_ss, z_rs, ag_ss, ag_rs, half_ss, half_rs, o_ss, o_rs, res_sem,
):
    dp, mp = lax.axis_index("dp"), lax.axis_index("mp")
    core, y, zh = dp % 2, (dp // 2) % RING, dp // 16
    rot = mp % RING
    row_core = mp // RING
    sib = (dp + 1 - 2 * core, mp)
    zother = ((1 - zh) * 16 + y * 2 + core, mp)
    factor = 1.0 / math.sqrt(ROWS * N_MP)

    def remote(src, dst, ss, rs, to):
        return pltpu.make_async_remote_copy(
            src_ref=src, dst_ref=dst, send_sem=ss, recv_sem=rs,
            device_id=to, device_id_type=MESH,
        )

    def await_copy(ref, sem):
        pltpu.make_async_copy(ref, ref, sem).wait()

    def along_y(hops):
        return (zh * 16 + ((y + hops + RING) % RING) * 2 + core, mp)

    def local_block(ring_index):
        return (ring_index + 2 * RING + rot) % RING

    def rows16(index):
        return pl.ds(pl.multiple_of(index * ROWS, ROWS), ROWS)

    started = []

    def start(copy):
        copy.start()
        started.append(copy)
        return copy

    own_loads = [
        pltpu.make_async_copy(src, mine.at[i], mine_sem.at[i])
        for i, src in enumerate((tok_hbm, cot_hbm))
    ]
    for copy in own_loads:
        copy.start()
    loads = [
        pltpu.make_async_copy(src, dst, load_sem.at[i])
        for i, (src, dst) in enumerate(((wg_hbm, wg), (wu_hbm, wu), (wd_hbm, wd)))
    ]
    for copy in loads:
        copy.start()

    peers = [sib, zother] + [along_y(hops) for hops in range(1, RING)]
    for k in range(1, N_MP):
        peers += [(dp, (mp + k) % N_MP), (sib[0], (mp + k) % N_MP)]
    barrier = pltpu.get_barrier_semaphore()
    for to in peers:
        pl.semaphore_signal(barrier, inc=1, device_id=to, device_id_type=MESH)
    pl.semaphore_wait(barrier, len(peers))

    worker = dp - core + row_core
    at_home = row_core == core
    gathers = []
    for i in range(2):
        own_loads[i].wait()
        target = rows.at[core, i, rows16(rot)]
        for k in range(1, N_MP):
            start(
                remote(
                    mine.at[i], target, gat_ss.at[i, k], gat_rs.at[i, core, rot],
                    (worker, (mp + k) % N_MP),
                )
            )
        stay = pltpu.make_async_copy(mine.at[i], target, gat_rs.at[i, core, rot])
        cross = remote(mine.at[i], target, gat_ss.at[i, 0], gat_rs.at[i, core, rot], sib)
        pl.when(at_home)(stay.start)
        pl.when(jnp.logical_not(at_home))(cross.start)
        gathers.append(cross)
        weights = ((wg_hbm, sg, 0), (wu_hbm, su, 1)) if i == 0 else ((wd_hbm, sd, 2),)
        for src, dst, j in weights:
            start(remote(src, dst, wsib_ss.at[j], wsib_rs.at[j], sib))

    def send_sums(array):
        for n, hops in enumerate((4, 3, -3, 2, -2, 1, -1)):
            index = local_block(y + hops)
            send[array, n] = encode(acc[array, rows16(index), :])
            start(
                remote(
                    send.at[array, n], recv.at[array, n],
                    rs_ss.at[array, n], rs_rs.at[array, n], along_y(hops),
                )
            )

    for i in range(2):
        for side in range(2):
            for b in range(RING):
                await_copy(rows.at[side, i, pl.ds(b * ROWS, ROWS)], gat_rs.at[i, side, b])
        near, far = rows[core, i], rows[1 - core, i]
        if i == 0:
            loads[0].wait()
            await_copy(sg, wsib_rs.at[0])
            acc[0] = dot(near, wg[...]) + dot(far, sg[...])
            send_sums(0)
            loads[1].wait()
            await_copy(su, wsib_rs.at[1])
            acc[1] = dot(near, wu[...]) + dot(far, su[...])
            send_sums(1)
        else:
            loads[2].wait()
            await_copy(sd, wsib_rs.at[2])
            acc[2] = dot_last(near, wd[...]) + dot_last(far, sd[...])
            send_sums(2)

    start(remote(rows.at[1 - core], other, oth_ss, oth_rs, sib))

    def collect(array):
        total = acc[array, rows16(local_block(y)), :]
        for n in range(RING - 1):
            await_copy(recv.at[array, n], rs_rs.at[array, n])
            total += decode(recv[array, n])
        sendz[array] = encode(total)
        start(remote(sendz.at[array], recvz.at[array], z_ss.at[array], z_rs.at[array], zother))
        return total

    gate, up, grad_hidden = collect(0), collect(1), collect(2)
    own = core * RING + local_block(y)
    hops_order = (1, -1, 2, -2, 3, -3, 4)

    def block_of(hops):
        return core * RING + local_block(y - hops)

    def spread(ref, which):
        for n, hops in enumerate(hops_order):
            start(
                remote(
                    ref.at[own], ref.at[own], ag_ss.at[which, n], ag_rs.at[which, n],
                    along_y(hops),
                )
            )

    await_copy(recvz.at[0], z_rs.at[0])
    await_copy(recvz.at[1], z_rs.at[1])
    gate += decode(recvz[0])
    up += decode(recvz[1])
    sig = jax.nn.sigmoid(gate)
    hid[own] = (gate * sig * up).astype(BF16)
    spread(hid, 0)
    await_copy(recvz.at[2], z_rs.at[2])
    grad_hidden += decode(recvz[2])
    gug[own, 0] = (grad_hidden * up * sig * (1.0 + gate * (1.0 - sig))).astype(BF16)
    gug[own, 1] = (grad_hidden * gate * sig).astype(BF16)
    spread(gug, 1)

    batches = ((0, 1, -1, 2, -2), (3, -3, 4))
    finals = []

    def arrive(ref, which, batch):
        for hops in batch:
            if hops:
                n = hops_order.index(hops)
                await_copy(ref.at[block_of(hops)], ag_rs.at[which, n])

    def deliver(which, side, batch, values):
        for n, hops in enumerate(batch):
            slot = (hops + RING) % RING * 2 + side
            index = block_of(hops)
            src, dst = part.at[which, slot], parts.at[which, mp]
            part[which, slot] = values[n * ROWS : (n + 1) * ROWS]
            to = (sib[0] if side else dp, index)
            copy = remote(src, dst, o_ss.at[which, slot], o_rs.at[which, mp], to)
            if side == 0:
                stay = pltpu.make_async_copy(src, dst, o_rs.at[which, mp])
                pl.when(index == mp)(stay.start)
                pl.when(index != mp)(copy.start)
                finals.append((copy, index))
            else:
                start(copy)

    def rows_of(ref, batch):
        return jnp.concatenate([ref[block_of(hops)] for hops in batch], axis=0)

    def my_half(ref):
        return ref.at[pl.ds(pl.multiple_of(core * RING, RING), RING)]

    def their_half(ref):
        return ref.at[pl.ds(pl.multiple_of((1 - core) * RING, RING), RING)]

    for batch in batches:
        arrive(hid, 0, batch)
        hidden = rows_of(hid, batch)
        for side, down_w in enumerate((wd, sd)):
            deliver(0, side, batch, dot(hidden, down_w[...]).astype(BF16))
    start(remote(my_half(hid), my_half(hid), half_ss.at[0], half_rs.at[0], sib))

    results = []

    def store(src, dst):
        copy = pltpu.make_async_copy(src, dst, res_sem.at[len(results)])
        copy.start()
        results.append(copy)

    await_copy(other, oth_rs)
    for i in range(2):
        full[i, pl.ds(pl.multiple_of(core * HALF, HALF), HALF), :] = rows[core, i]
        full[i, pl.ds(pl.multiple_of((1 - core) * HALF, HALF), HALF), :] = other[i]

    def grads_tokens(batch):
        arrive(gug, 1, batch)
        grad_gate = jnp.concatenate([gug[block_of(hops), 0] for hops in batch], axis=0)
        grad_up = jnp.concatenate([gug[block_of(hops), 1] for hops in batch], axis=0)
        for side, (gate_w, up_w) in enumerate(((wg, wu), (sg, su))):
            value = dot_last(grad_gate, gate_w[...]) + dot_last(grad_up, up_w[...])
            deliver(1, side, batch, value.astype(BF16))

    grads_tokens(batches[0])
    await_copy(their_half(hid), half_rs.at[0])
    dgrad[...] = (dot_first(hid[...].reshape(2 * HALF, -1), full[1]) * factor).astype(BF16)
    store(dgrad, dgrad_hbm)
    grads_tokens(batches[1])

    start(remote(my_half(gug), my_half(gug), half_ss.at[1], half_rs.at[1], sib))
    await_copy(their_half(gug), half_rs.at[1])
    grad_gate = gug[:, 0].reshape(2 * HALF, -1)
    grad_up = gug[:, 1].reshape(2 * HALF, -1)
    ggrad[...] = (dot_first(full[0], grad_gate) * factor).astype(BF16)
    store(ggrad, ggrad_hbm)
    ugrad[...] = (dot_first(full[0], grad_up) * factor).astype(BF16)
    store(ugrad, ugrad_hbm)

    for which, target in enumerate((out_hbm, tgrad_hbm)):
        total = jnp.zeros((ROWS, 256), F32)
        for k in range(N_MP):
            await_copy(parts.at[which, k], o_rs.at[which, k])
            total += parts[which, k].astype(F32)
        small[which] = total.astype(BF16)
        store(small.at[which], target)

    for copy in started:
        copy.wait_send()
    for i in range(2):
        pl.when(jnp.logical_not(at_home))(gathers[i].wait_send)
    for copy, index in finals:
        pl.when(index != mp)(copy.wait_send)
    for copy in results:
        copy.wait()


def copy_out(*refs):
    sources, targets, staged, sems = refs[:5], refs[5:10], refs[10:15], refs[15]
    loads = [
        pltpu.make_async_copy(src, mid, sems.at[0, i])
        for i, (src, mid) in enumerate(zip(sources, staged))
    ]
    stores = [
        pltpu.make_async_copy(mid, dst, sems.at[1, i])
        for i, (mid, dst) in enumerate(zip(staged, targets))
    ]
    for copy in loads:
        copy.start()
    for load, store in zip(loads, stores):
        load.wait()
        store.start()
    for copy in stores:
        copy.wait()


def on_device(tokens, gate_weight, up_weight, down_weight, cotangent):
    count, width = tokens.shape
    units = gate_weight.shape[1]
    hbm = pl.BlockSpec(memory_space=pltpu.HBM)
    dma = pltpu.SemaphoreType.DMA

    def vmem(*shape, dtype=BF16):
        return pltpu.VMEM(shape, dtype)

    shapes = (
        jax.ShapeDtypeStruct((count, width), BF16),
        jax.ShapeDtypeStruct((count, width), BF16),
        jax.ShapeDtypeStruct((width, units), BF16),
        jax.ShapeDtypeStruct((width, units), BF16),
        jax.ShapeDtypeStruct((units, width), BF16),
    )
    results = pl.pallas_call(
        kernel,
        out_shape=shapes,
        in_specs=[hbm] * 5,
        out_specs=[hbm] * 5,
        scratch_shapes=[
            vmem(width, units), vmem(width, units), vmem(units, width),
            vmem(width, units), vmem(width, units), vmem(units, width),
            vmem(2, ROWS, width), vmem(2, 2, HALF, width), vmem(2, HALF, width),
            vmem(2, 2 * HALF, width), vmem(3, HALF, units, dtype=F32),
            vmem(3, RING - 1, ROWS, units), vmem(3, RING - 1, ROWS, units),
            vmem(3, ROWS, units), vmem(3, ROWS, units),
            vmem(N_MP, ROWS, units), vmem(N_MP, 2, ROWS, units),
            vmem(2, N_MP, ROWS, width), vmem(2, N_MP, ROWS, width), vmem(2, ROWS, width),
            vmem(width, units), vmem(width, units), vmem(units, width),
            dma((3,)), dma((2,)), dma((3,)), dma((3,)), dma((2, N_MP)), dma((2, 2, RING)),
            dma(()), dma(()),
            dma((3, RING - 1)), dma((3, RING - 1)), dma((3,)), dma((3,)),
            dma((2, RING - 1)), dma((2, RING - 1)), dma((2,)), dma((2,)),
            dma((2, N_MP)), dma((2, N_MP)), dma((5,)),
        ],
        compiler_params=pltpu.CompilerParams(
            collective_id=0, has_side_effects=True, vmem_limit_bytes=VMEM_LIMIT
        ),
    )(tokens, cotangent, gate_weight, up_weight, down_weight)
    return pl.pallas_call(
        copy_out,
        out_shape=shapes,
        in_specs=[hbm] * 5,
        out_specs=[hbm] * 5,
        scratch_shapes=[pltpu.VMEM(s.shape, s.dtype) for s in shapes] + [dma((2, 5))],
        compiler_params=pltpu.CompilerParams(vmem_limit_bytes=VMEM_LIMIT),
    )(*results)


def solution(mesh):
    in_specs = (P("mp", "dp"), P("dp", "mp"), P("dp", "mp"), P("mp", "dp"), P("mp", "dp"))
    out_specs = (P("mp", "dp"), P("mp", "dp"), P("dp", "mp"), P("dp", "mp"), P("mp", "dp"))
    return jax.shard_map(
        on_device, mesh=mesh, in_specs=in_specs, out_specs=out_specs, check_vma=False
    )
```

```python
import math

import jax
import jax.numpy as jnp
from jax import lax
from jax.experimental import pallas as pl
from jax.experimental.pallas import tpu as pltpu
from jax.sharding import PartitionSpec as P

MESH = pl.DeviceIdType.MESH
F32 = jnp.float32
BF16 = jnp.bfloat16
RING = 8
ROWS = 16
HALF = RING * ROWS
N_MP = 16
VMEM_LIMIT = 62 * 2**20
CODE_SCALE = float(2**18)


def encode(x):
    x = x * CODE_SCALE
    return (x * x * (x * jnp.abs(x))).astype(BF16)


def decode(code):
    y = code.astype(F32)
    root = lax.rsqrt(lax.rsqrt(jnp.abs(y))) * (1.0 / CODE_SCALE)
    return jnp.where(y < 0, -root, root)


def dot(left, right):
    return jnp.dot(left, right, preferred_element_type=F32)


def dot_last(left, right):
    return lax.dot_general(left, right, (((1,), (1,)), ((), ())), preferred_element_type=F32)


def dot_first(left, right):
    return lax.dot_general(left, right, (((0,), (0,)), ((), ())), preferred_element_type=F32)


def kernel(
    tok_hbm, cot_hbm, wg_hbm, wu_hbm, wd_hbm,
    out_hbm, tgrad_hbm, ggrad_hbm, ugrad_hbm, dgrad_hbm,
    wg, wu, wd, sg, su, sd,
    mine, rows, other, full, acc, send, recv, sendz, recvz,
    hgu, part, parts, small, ggrad, ugrad, dgrad,
    load_sem, mine_sem, wsib_ss, wsib_rs, gat_ss, gat_rs, oth_ss, oth_rs,
    rs_ss, rs_rs, z_ss, z_rs, ag_ss, ag_rs, half_ss, half_rs, o_ss, o_rs, res_sem,
):
    dp, mp = lax.axis_index("dp"), lax.axis_index("mp")
    core, y, zh = dp % 2, (dp // 2) % RING, dp // 16
    rot = mp % RING
    row_core = mp // RING
    sib = (dp + 1 - 2 * core, mp)
    zother = ((1 - zh) * 16 + y * 2 + core, mp)
    factor = 1.0 / math.sqrt(ROWS * N_MP)

    def remote(src, dst, ss, rs, to):
        return pltpu.make_async_remote_copy(
            src_ref=src, dst_ref=dst, send_sem=ss, recv_sem=rs,
            device_id=to, device_id_type=MESH,
        )

    def await_copy(ref, sem):
        pltpu.make_async_copy(ref, ref, sem).wait()

    def along_y(hops):
        return (zh * 16 + ((y + hops + RING) % RING) * 2 + core, mp)

    def local_block(ring_index):
        return (ring_index + 2 * RING + rot) % RING

    def rows16(index):
        return pl.ds(pl.multiple_of(index * ROWS, ROWS), ROWS)

    started = []

    def start(copy):
        copy.start()
        started.append(copy)
        return copy

    own_loads = [
        pltpu.make_async_copy(src, mine.at[i], mine_sem.at[i])
        for i, src in enumerate((tok_hbm, cot_hbm))
    ]
    for copy in own_loads:
        copy.start()
    loads = [
        pltpu.make_async_copy(src, dst, load_sem.at[i])
        for i, (src, dst) in enumerate(((wg_hbm, wg), (wu_hbm, wu), (wd_hbm, wd)))
    ]
    for copy in loads:
        copy.start()

    peers = [sib, zother] + [along_y(hops) for hops in (1, -1, 2, -2)]
    for k in range(1, N_MP):
        peers += [(dp, (mp + k) % N_MP), (sib[0], (mp + k) % N_MP)]
    barrier = pltpu.get_barrier_semaphore()
    for to in peers:
        pl.semaphore_signal(barrier, inc=1, device_id=to, device_id_type=MESH)
    pl.semaphore_wait(barrier, len(peers))

    worker = dp - core + row_core
    at_home = row_core == core
    for copy in own_loads:
        copy.wait()
    target = rows.at[core, rot]
    for k in range(1, N_MP):
        start(
            remote(
                mine, target, gat_ss.at[k], gat_rs.at[core, rot],
                (worker, (mp + k) % N_MP),
            )
        )
    stay = pltpu.make_async_copy(mine, target, gat_rs.at[core, rot])
    cross = remote(mine, target, gat_ss.at[0], gat_rs.at[core, rot], sib)
    pl.when(at_home)(stay.start)
    pl.when(jnp.logical_not(at_home))(cross.start)
    for j, (src, dst) in enumerate(((wg_hbm, sg), (wu_hbm, su), (wd_hbm, sd))):
        start(remote(src, dst, wsib_ss.at[j], wsib_rs.at[j], sib))

    for copy in loads:
        copy.wait()
    for j, dst in enumerate((sg, su, sd)):
        await_copy(dst, wsib_rs.at[j])
    for side in range(2):
        for b in range(RING):
            await_copy(rows.at[side, b], gat_rs.at[side, b])
    near = rows[core].reshape(RING, 2, ROWS, -1)
    far = rows[1 - core].reshape(RING, 2, ROWS, -1)
    near_tok, near_cot = near[:, 0].reshape(HALF, -1), near[:, 1].reshape(HALF, -1)
    far_tok, far_cot = far[:, 0].reshape(HALF, -1), far[:, 1].reshape(HALF, -1)
    acc[0] = dot(near_tok, wg[...]) + dot(far_tok, sg[...])
    acc[1] = dot(near_tok, wu[...]) + dot(far_tok, su[...])
    acc[2] = dot_last(near_cot, wd[...]) + dot_last(far_cot, sd[...])

    def block_sum(hops):
        return acc[:, rows16(local_block(y + hops)), :]

    def send_sums(slot, lane, arrays, hops):
        start(
            remote(
                send.at[slot, arrays], recv.at[slot, arrays],
                rs_ss.at[lane], rs_rs.at[lane], along_y(hops),
            )
        )

    first, rest, whole = pl.ds(0, 1), pl.ds(1, 2), pl.ds(0, 3)
    send[0] = encode(block_sum(4))
    send_sums(0, 0, first, -2)
    send_sums(0, 1, rest, 2)
    send[1] = encode(block_sum(3))
    send_sums(1, 2, whole, 1)
    send[2] = encode(block_sum(-3))
    send_sums(2, 3, whole, -1)
    send[3] = encode(block_sum(1))
    send_sums(3, 4, whole, 1)
    send[4] = encode(block_sum(-1))
    send_sums(4, 5, whole, -1)
    start(remote(rows.at[1 - core], other, oth_ss, oth_rs, sib))
    await_copy(recv.at[1], rs_rs.at[2])
    await_copy(recv.at[0, rest], rs_rs.at[1])
    acc[:, rows16(local_block(y + 2)), :] += decode(recv[1])
    send[5, 0] = encode(acc[0, rows16(local_block(y + 2)), :])
    send[5, 1:] = encode(acc[1:, rows16(local_block(y + 2)), :] + decode(recv[0, 1:]))
    send_sums(5, 6, whole, 2)
    await_copy(recv.at[2], rs_rs.at[3])
    await_copy(recv.at[0, first], rs_rs.at[0])
    acc[:, rows16(local_block(y - 2)), :] += decode(recv[2])
    send[6, 0] = encode(acc[0, rows16(local_block(y - 2)), :] + decode(recv[0, 0]))
    send[6, 1:] = encode(acc[1:, rows16(local_block(y - 2)), :])
    send_sums(6, 7, whole, -2)
    total = block_sum(0)
    for slot, lane in ((3, 4), (4, 5), (5, 6), (6, 7)):
        await_copy(recv.at[slot], rs_rs.at[lane])
        total += decode(recv[slot])
    sendz[...] = encode(total)
    start(remote(sendz, recvz, z_ss, z_rs, zother))
    await_copy(recvz, z_rs)
    total += decode(recvz[...])
    gate, up, grad_hidden = total[0], total[1], total[2]
    sig = jax.nn.sigmoid(gate)

    def block_of(hops):
        return core * RING + local_block(y - hops)

    own = block_of(0)
    hgu[own, 0] = (gate * sig * up).astype(BF16)
    hgu[own, 1] = (grad_hidden * up * sig * (1.0 + gate * (1.0 - sig))).astype(BF16)
    hgu[own, 2] = (grad_hidden * gate * sig).astype(BF16)

    def spread(lane, arrays, source, hops):
        ref = hgu.at[block_of(source), arrays]
        start(remote(ref, ref, ag_ss.at[lane], ag_rs.at[lane], along_y(hops)))

    def arrive(lane, arrays, source):
        await_copy(hgu.at[block_of(source), arrays], ag_rs.at[lane])

    spread(0, whole, 0, 2)
    spread(1, whole, 0, -2)
    spread(2, whole, 0, 1)
    spread(3, whole, 0, -1)
    arrive(0, whole, 2)
    spread(4, whole, 2, 1)
    spread(6, first, 2, 2)
    arrive(1, whole, -2)
    spread(5, whole, -2, -1)
    spread(7, rest, -2, -2)
    arrive(2, whole, 1)
    arrive(3, whole, -1)

    finals = []

    def multiply(batch):
        blocks = [hgu[block_of(hops)] for hops in batch]
        hidden, grad_gate, grad_up = (
            jnp.concatenate([block[array] for block in blocks], axis=0) for array in range(3)
        )
        for side, (gate_w, up_w, down_w) in enumerate(((wg, wu, wd), (sg, su, sd))):
            values = (
                dot(hidden, down_w[...]),
                dot_last(grad_gate, gate_w[...]) + dot_last(grad_up, up_w[...]),
            )
            for n, hops in enumerate(batch):
                slot = (hops + RING) % RING * 2 + side
                index = block_of(hops)
                for which in range(2):
                    value = values[which][n * ROWS : (n + 1) * ROWS]
                    part[slot, which] = value.astype(BF16)
                src, dst = part.at[slot], parts.at[mp]
                copy = remote(
                    src, dst, o_ss.at[slot], o_rs.at[mp], (sib[0] if side else dp, index)
                )
                if side == 0:
                    stay = pltpu.make_async_copy(src, dst, o_rs.at[mp])
                    pl.when(index == mp)(stay.start)
                    pl.when(index != mp)(copy.start)
                    finals.append((copy, index))
                else:
                    start(copy)

    multiply((0, 1, -1, 2, -2))
    arrive(4, whole, 3)
    arrive(5, whole, -3)
    arrive(6, first, 4)
    arrive(7, rest, -4)
    multiply((3, -3, 4))

    my_half = hgu.at[pl.ds(pl.multiple_of(core * RING, RING), RING)]
    their_half = hgu.at[pl.ds(pl.multiple_of((1 - core) * RING, RING), RING)]
    start(remote(my_half, my_half, half_ss, half_rs, sib))
    await_copy(other, oth_rs)
    theirs = other[...]
    for i in range(2):
        full[i, pl.ds(pl.multiple_of(core * HALF, HALF), HALF), :] = (
            rows[core][:, i].reshape(HALF, -1)
        )
        full[i, pl.ds(pl.multiple_of((1 - core) * HALF, HALF), HALF), :] = (
            theirs[:, i].reshape(HALF, -1)
        )

    results = []

    def store(src, dst):
        copy = pltpu.make_async_copy(src, dst, res_sem.at[len(results)])
        copy.start()
        results.append(copy)

    await_copy(their_half, half_rs)
    hidden = hgu[:, 0].reshape(2 * HALF, -1)
    grad_gate = hgu[:, 1].reshape(2 * HALF, -1)
    grad_up = hgu[:, 2].reshape(2 * HALF, -1)
    ggrad[...] = (dot_first(full[0], grad_gate) * factor).astype(BF16)
    store(ggrad, ggrad_hbm)
    ugrad[...] = (dot_first(full[0], grad_up) * factor).astype(BF16)
    store(ugrad, ugrad_hbm)
    dgrad[...] = (dot_first(hidden, full[1]) * factor).astype(BF16)
    store(dgrad, dgrad_hbm)

    total = jnp.zeros((2, ROWS, 256), F32)
    for k in range(N_MP):
        await_copy(parts.at[k], o_rs.at[k])
        total += parts[k].astype(F32)
    small[...] = total.astype(BF16)
    store(small.at[0], out_hbm)
    store(small.at[1], tgrad_hbm)

    for copy in started:
        copy.wait_send()
    pl.when(jnp.logical_not(at_home))(cross.wait_send)
    for copy, index in finals:
        pl.when(index != mp)(copy.wait_send)
    for copy in results:
        copy.wait()


def copy_out(*refs):
    sources, targets, staged, sems = refs[:5], refs[5:10], refs[10:15], refs[15]
    loads = [
        pltpu.make_async_copy(src, mid, sems.at[0, i])
        for i, (src, mid) in enumerate(zip(sources, staged))
    ]
    stores = [
        pltpu.make_async_copy(mid, dst, sems.at[1, i])
        for i, (mid, dst) in enumerate(zip(staged, targets))
    ]
    for copy in loads:
        copy.start()
    for load, store in zip(loads, stores):
        load.wait()
        store.start()
    for copy in stores:
        copy.wait()


def on_device(tokens, gate_weight, up_weight, down_weight, cotangent):
    count, width = tokens.shape
    units = gate_weight.shape[1]
    hbm = pl.BlockSpec(memory_space=pltpu.HBM)
    dma = pltpu.SemaphoreType.DMA

    def vmem(*shape, dtype=BF16):
        return pltpu.VMEM(shape, dtype)

    shapes = (
        jax.ShapeDtypeStruct((count, width), BF16),
        jax.ShapeDtypeStruct((count, width), BF16),
        jax.ShapeDtypeStruct((width, units), BF16),
        jax.ShapeDtypeStruct((width, units), BF16),
        jax.ShapeDtypeStruct((units, width), BF16),
    )
    results = pl.pallas_call(
        kernel,
        out_shape=shapes,
        in_specs=[hbm] * 5,
        out_specs=[hbm] * 5,
        scratch_shapes=[
            vmem(width, units), vmem(width, units), vmem(units, width),
            vmem(width, units), vmem(width, units), vmem(units, width),
            vmem(2, ROWS, width), vmem(2, RING, 2, ROWS, width), vmem(RING, 2, ROWS, width),
            vmem(2, 2 * HALF, width), vmem(3, HALF, units, dtype=F32),
            vmem(7, 3, ROWS, units), vmem(7, 3, ROWS, units),
            vmem(3, ROWS, units), vmem(3, ROWS, units),
            vmem(N_MP, 3, ROWS, units),
            vmem(N_MP, 2, ROWS, width), vmem(N_MP, 2, ROWS, width), vmem(2, ROWS, width),
            vmem(width, units), vmem(width, units), vmem(units, width),
            dma((3,)), dma((2,)), dma((3,)), dma((3,)), dma((N_MP,)), dma((2, RING)),
            dma(()), dma(()), dma((8,)), dma((8,)), dma(()), dma(()),
            dma((8,)), dma((8,)), dma(()), dma(()), dma((N_MP,)), dma((N_MP,)), dma((5,)),
        ],
        compiler_params=pltpu.CompilerParams(
            collective_id=0, has_side_effects=True, vmem_limit_bytes=VMEM_LIMIT
        ),
    )(tokens, cotangent, gate_weight, up_weight, down_weight)
    return pl.pallas_call(
        copy_out,
        out_shape=shapes,
        in_specs=[hbm] * 5,
        out_specs=[hbm] * 5,
        scratch_shapes=[pltpu.VMEM(s.shape, s.dtype) for s in shapes] + [dma((2, 5))],
        compiler_params=pltpu.CompilerParams(vmem_limit_bytes=VMEM_LIMIT),
    )(*results)


def solution(mesh):
    in_specs = (P("mp", "dp"), P("dp", "mp"), P("dp", "mp"), P("mp", "dp"), P("mp", "dp"))
    out_specs = (P("mp", "dp"), P("mp", "dp"), P("dp", "mp"), P("dp", "mp"), P("mp", "dp"))
    return jax.shard_map(
        on_device, mesh=mesh, in_specs=in_specs, out_specs=out_specs, check_vma=False
    )
```

```python
import math

import jax
import jax.numpy as jnp
from jax import lax
from jax.experimental import pallas as pl
from jax.experimental.pallas import tpu as pltpu
from jax.sharding import PartitionSpec as P

MESH = pl.DeviceIdType.MESH
F32 = jnp.float32
BF16 = jnp.bfloat16
RING = 8
ROWS = 16
HALF = RING * ROWS
N_MP = 16
VMEM_LIMIT = 62 * 2**20
CODE_SCALE = float(2**18)


def encode(x):
    x = x * CODE_SCALE
    return (x * x * (x * jnp.abs(x))).astype(BF16)


def decode(code):
    y = code.astype(F32)
    root = lax.rsqrt(lax.rsqrt(jnp.abs(y))) * (1.0 / CODE_SCALE)
    return jnp.where(y < 0, -root, root)


def dot(left, right):
    return jnp.dot(left, right, preferred_element_type=F32)


def dot_last(left, right):
    return lax.dot_general(left, right, (((1,), (1,)), ((), ())), preferred_element_type=F32)


def dot_first(left, right):
    return lax.dot_general(left, right, (((0,), (0,)), ((), ())), preferred_element_type=F32)


def kernel(
    tok_hbm, cot_hbm, wg_hbm, wu_hbm, wd_hbm,
    out_hbm, tgrad_hbm, ggrad_hbm, ugrad_hbm, dgrad_hbm,
    wg, wu, wd, sg, su, sd,
    mine, rows, other, full, acc, send, recv, sendz, recvz,
    hgu, part, parts, small, ggrad, ugrad, dgrad,
    load_sem, mine_sem, wsib_ss, wsib_rs, gat_ss, gat_rs, oth_ss, oth_rs,
    rs_ss, rs_rs, z_ss, z_rs, ag_ss, ag_rs, half_ss, half_rs, o_ss, o_rs, res_sem,
):
    dp, mp = lax.axis_index("dp"), lax.axis_index("mp")
    core, y, zh = dp % 2, (dp // 2) % RING, dp // 16
    rot = mp % RING
    row_core = mp // RING
    sib = (dp + 1 - 2 * core, mp)
    zother = ((1 - zh) * 16 + y * 2 + core, mp)
    factor = 1.0 / math.sqrt(ROWS * N_MP)

    def remote(src, dst, ss, rs, to):
        return pltpu.make_async_remote_copy(
            src_ref=src, dst_ref=dst, send_sem=ss, recv_sem=rs,
            device_id=to, device_id_type=MESH,
        )

    def await_copy(ref, sem):
        pltpu.make_async_copy(ref, ref, sem).wait()

    def along_y(hops):
        return (zh * 16 + ((y + hops + RING) % RING) * 2 + core, mp)

    def local_block(ring_index):
        return (ring_index + 2 * RING + rot) % RING

    def rows16(index):
        return pl.ds(pl.multiple_of(index * ROWS, ROWS), ROWS)

    started = []

    def start(copy):
        copy.start()
        started.append(copy)
        return copy

    own_loads = [
        pltpu.make_async_copy(src, mine.at[i], mine_sem.at[i])
        for i, src in enumerate((tok_hbm, cot_hbm))
    ]
    for copy in own_loads:
        copy.start()
    loads = [
        pltpu.make_async_copy(src, dst, load_sem.at[i])
        for i, (src, dst) in enumerate(((wg_hbm, wg), (wu_hbm, wu), (wd_hbm, wd)))
    ]
    for copy in loads:
        copy.start()

    peers = [sib, zother] + [along_y(hops) for hops in (1, -1, 2, -2)]
    for k in range(1, N_MP):
        peers += [(dp, (mp + k) % N_MP), (sib[0], (mp + k) % N_MP)]
    barrier = pltpu.get_barrier_semaphore()
    for to in peers:
        pl.semaphore_signal(barrier, inc=1, device_id=to, device_id_type=MESH)
    pl.semaphore_wait(barrier, len(peers))

    worker = dp - core + row_core
    at_home = row_core == core
    for copy in own_loads:
        copy.wait()
    target = rows.at[core, rot]
    for k in range(1, N_MP):
        start(
            remote(
                mine, target, gat_ss.at[k], gat_rs.at[core, rot],
                (worker, (mp + k) % N_MP),
            )
        )
    stay = pltpu.make_async_copy(mine, target, gat_rs.at[core, rot])
    cross = remote(mine, target, gat_ss.at[0], gat_rs.at[core, rot], sib)
    pl.when(at_home)(stay.start)
    pl.when(jnp.logical_not(at_home))(cross.start)
    for j, (src, dst) in enumerate(((wg_hbm, sg), (wu_hbm, su), (wd_hbm, sd))):
        start(remote(src, dst, wsib_ss.at[j], wsib_rs.at[j], sib))

    for copy in loads:
        copy.wait()
    for j, dst in enumerate((sg, su, sd)):
        await_copy(dst, wsib_rs.at[j])
    for side in range(2):
        for b in range(RING):
            await_copy(rows.at[side, b], gat_rs.at[side, b])
    near = rows[core].reshape(RING, 2, ROWS, -1)
    far = rows[1 - core].reshape(RING, 2, ROWS, -1)
    near_tok, near_cot = near[:, 0].reshape(HALF, -1), near[:, 1].reshape(HALF, -1)
    far_tok, far_cot = far[:, 0].reshape(HALF, -1), far[:, 1].reshape(HALF, -1)
    acc[0] = dot(near_tok, wg[...]) + dot(far_tok, sg[...])
    acc[1] = dot(near_tok, wu[...]) + dot(far_tok, su[...])
    acc[2] = dot_last(near_cot, wd[...]) + dot_last(far_cot, sd[...])

    def block_sum(array, hops):
        return acc[array, rows16(local_block(y + hops)), :]

    def send_sums(slot, array, value, hops):
        send[slot, array] = encode(value)
        start(
            remote(
                send.at[slot, array], recv.at[slot, array],
                rs_ss.at[slot, array], rs_rs.at[slot, array], along_y(hops),
            )
        )

    def received(slot, array):
        await_copy(recv.at[slot, array], rs_rs.at[slot, array])
        return decode(recv[slot, array])

    far_side = (-2, 2, 2)
    for array in range(3):
        send_sums(0, array, block_sum(array, 4), far_side[array])
        send_sums(1, array, block_sum(array, 3), 1)
        send_sums(2, array, block_sum(array, -3), -1)
    for array in range(3):
        send_sums(3, array, block_sum(array, 1), 1)
        send_sums(4, array, block_sum(array, -1), -1)
    for array in range(3):
        for slot, hops in ((1, 2), (2, -2)):
            value = block_sum(array, hops) + received(slot, array)
            if far_side[array] == hops:
                value += received(0, array)
            send_sums(slot + 4, array, value, hops)
    start(remote(rows.at[1 - core], other, oth_ss, oth_rs, sib))
    totals = []
    for array in range(3):
        total = block_sum(array, 0)
        for slot in (3, 4, 5, 6):
            total += received(slot, array)
        sendz[array] = encode(total)
        start(remote(sendz.at[array], recvz.at[array], z_ss.at[array], z_rs.at[array], zother))
        totals.append(total)

    def swapped(array):
        await_copy(recvz.at[array], z_rs.at[array])
        return totals[array] + decode(recvz[array])

    def block_of(hops):
        return core * RING + local_block(y - hops)

    groups = (slice(0, 1), slice(1, 3))

    def spread(lane, group, source, hops):
        ref = hgu.at[block_of(source), groups[group]]
        start(remote(ref, ref, ag_ss.at[lane, group], ag_rs.at[lane, group], along_y(hops)))

    def arrive(lane, group, source):
        await_copy(hgu.at[block_of(source), groups[group]], ag_rs.at[lane, group])

    own = block_of(0)
    gate, up = swapped(0), swapped(1)
    sig = jax.nn.sigmoid(gate)
    hgu[own, 0] = (gate * sig * up).astype(BF16)
    for lane, hops in enumerate((2, -2, 1, -1)):
        spread(lane, 0, 0, hops)
    grad_hidden = swapped(2)
    hgu[own, 1] = (grad_hidden * up * sig * (1.0 + gate * (1.0 - sig))).astype(BF16)
    hgu[own, 2] = (grad_hidden * gate * sig).astype(BF16)
    for lane, hops in enumerate((2, -2, 1, -1)):
        spread(lane, 1, 0, hops)
    for group in range(2):
        for lane, hops in ((0, 2), (1, -2)):
            arrive(lane, group, hops)
            spread(lane + 4, group, hops, hops // 2)
            if (hops > 0) == (group == 0):
                spread(6, group, hops, hops)
    for group in range(2):
        arrive(2, group, 1)
        arrive(3, group, -1)

    finals = []

    def multiply(batch):
        blocks = [hgu[block_of(hops)] for hops in batch]
        hidden, grad_gate, grad_up = (
            jnp.concatenate([block[array] for block in blocks], axis=0) for array in range(3)
        )
        for side, (gate_w, up_w, down_w) in enumerate(((wg, wu, wd), (sg, su, sd))):
            values = (
                dot(hidden, down_w[...]),
                dot_last(grad_gate, gate_w[...]) + dot_last(grad_up, up_w[...]),
            )
            for n, hops in enumerate(batch):
                slot = (hops + RING) % RING * 2 + side
                index = block_of(hops)
                for which in range(2):
                    value = values[which][n * ROWS : (n + 1) * ROWS]
                    part[slot, which] = value.astype(BF16)
                src, dst = part.at[slot], parts.at[mp]
                copy = remote(
                    src, dst, o_ss.at[slot], o_rs.at[mp], (sib[0] if side else dp, index)
                )
                if side == 0:
                    stay = pltpu.make_async_copy(src, dst, o_rs.at[mp])
                    pl.when(index == mp)(stay.start)
                    pl.when(index != mp)(copy.start)
                    finals.append((copy, index))
                else:
                    start(copy)

    multiply((0, 1, -1, 2, -2))
    for group in range(2):
        arrive(4, group, 3)
        arrive(5, group, -3)
        arrive(6, group, 4)
    multiply((3, -3, 4))

    my_half = hgu.at[pl.ds(pl.multiple_of(core * RING, RING), RING)]
    their_half = hgu.at[pl.ds(pl.multiple_of((1 - core) * RING, RING), RING)]
    start(remote(my_half, my_half, half_ss, half_rs, sib))
    await_copy(other, oth_rs)
    theirs = other[...]
    for i in range(2):
        full[i, pl.ds(pl.multiple_of(core * HALF, HALF), HALF), :] = (
            rows[core][:, i].reshape(HALF, -1)
        )
        full[i, pl.ds(pl.multiple_of((1 - core) * HALF, HALF), HALF), :] = (
            theirs[:, i].reshape(HALF, -1)
        )

    results = []

    def store(src, dst):
        copy = pltpu.make_async_copy(src, dst, res_sem.at[len(results)])
        copy.start()
        results.append(copy)

    await_copy(their_half, half_rs)
    hidden = hgu[:, 0].reshape(2 * HALF, -1)
    grad_gate = hgu[:, 1].reshape(2 * HALF, -1)
    grad_up = hgu[:, 2].reshape(2 * HALF, -1)
    ggrad[...] = (dot_first(full[0], grad_gate) * factor).astype(BF16)
    store(ggrad, ggrad_hbm)
    ugrad[...] = (dot_first(full[0], grad_up) * factor).astype(BF16)
    store(ugrad, ugrad_hbm)
    dgrad[...] = (dot_first(hidden, full[1]) * factor).astype(BF16)
    store(dgrad, dgrad_hbm)

    total = jnp.zeros((2, ROWS, 256), F32)
    for k in range(N_MP):
        await_copy(parts.at[k], o_rs.at[k])
        total += parts[k].astype(F32)
    small[...] = total.astype(BF16)
    store(small.at[0], out_hbm)
    store(small.at[1], tgrad_hbm)

    for copy in started:
        copy.wait_send()
    pl.when(jnp.logical_not(at_home))(cross.wait_send)
    for copy, index in finals:
        pl.when(index != mp)(copy.wait_send)
    for copy in results:
        copy.wait()


def copy_out(*refs):
    sources, targets, staged, sems = refs[:5], refs[5:10], refs[10:15], refs[15]
    loads = [
        pltpu.make_async_copy(src, mid, sems.at[0, i])
        for i, (src, mid) in enumerate(zip(sources, staged))
    ]
    stores = [
        pltpu.make_async_copy(mid, dst, sems.at[1, i])
        for i, (mid, dst) in enumerate(zip(staged, targets))
    ]
    for copy in loads:
        copy.start()
    for load, store in zip(loads, stores):
        load.wait()
        store.start()
    for copy in stores:
        copy.wait()


def on_device(tokens, gate_weight, up_weight, down_weight, cotangent):
    count, width = tokens.shape
    units = gate_weight.shape[1]
    hbm = pl.BlockSpec(memory_space=pltpu.HBM)
    dma = pltpu.SemaphoreType.DMA

    def vmem(*shape, dtype=BF16):
        return pltpu.VMEM(shape, dtype)

    shapes = (
        jax.ShapeDtypeStruct((count, width), BF16),
        jax.ShapeDtypeStruct((count, width), BF16),
        jax.ShapeDtypeStruct((width, units), BF16),
        jax.ShapeDtypeStruct((width, units), BF16),
        jax.ShapeDtypeStruct((units, width), BF16),
    )
    results = pl.pallas_call(
        kernel,
        out_shape=shapes,
        in_specs=[hbm] * 5,
        out_specs=[hbm] * 5,
        scratch_shapes=[
            vmem(width, units), vmem(width, units), vmem(units, width),
            vmem(width, units), vmem(width, units), vmem(units, width),
            vmem(2, ROWS, width), vmem(2, RING, 2, ROWS, width), vmem(RING, 2, ROWS, width),
            vmem(2, 2 * HALF, width), vmem(3, HALF, units, dtype=F32),
            vmem(7, 3, ROWS, units), vmem(7, 3, ROWS, units),
            vmem(3, ROWS, units), vmem(3, ROWS, units),
            vmem(N_MP, 3, ROWS, units),
            vmem(N_MP, 2, ROWS, width), vmem(N_MP, 2, ROWS, width), vmem(2, ROWS, width),
            vmem(width, units), vmem(width, units), vmem(units, width),
            dma((3,)), dma((2,)), dma((3,)), dma((3,)), dma((N_MP,)), dma((2, RING)),
            dma(()), dma(()), dma((7, 3)), dma((7, 3)), dma((3,)), dma((3,)),
            dma((7, 2)), dma((7, 2)), dma(()), dma(()), dma((N_MP,)), dma((N_MP,)), dma((5,)),
        ],
        compiler_params=pltpu.CompilerParams(
            collective_id=0, has_side_effects=True, vmem_limit_bytes=VMEM_LIMIT
        ),
    )(tokens, cotangent, gate_weight, up_weight, down_weight)
    return pl.pallas_call(
        copy_out,
        out_shape=shapes,
        in_specs=[hbm] * 5,
        out_specs=[hbm] * 5,
        scratch_shapes=[pltpu.VMEM(s.shape, s.dtype) for s in shapes] + [dma((2, 5))],
        compiler_params=pltpu.CompilerParams(vmem_limit_bytes=VMEM_LIMIT),
    )(*results)


def solution(mesh):
    in_specs = (P("mp", "dp"), P("dp", "mp"), P("dp", "mp"), P("mp", "dp"), P("mp", "dp"))
    out_specs = (P("mp", "dp"), P("mp", "dp"), P("dp", "mp"), P("dp", "mp"), P("mp", "dp"))
    return jax.shard_map(
        on_device, mesh=mesh, in_specs=in_specs, out_specs=out_specs, check_vma=False
    )
```

```python
import math

import jax
import jax.numpy as jnp
from jax import lax
from jax.experimental import pallas as pl
from jax.experimental.pallas import tpu as pltpu
from jax.sharding import PartitionSpec as P

MESH = pl.DeviceIdType.MESH
F32 = jnp.float32
BF16 = jnp.bfloat16
RING = 8
ROWS = 16
HALF = RING * ROWS
N_MP = 16
VMEM_LIMIT = 62 * 2**20
CODE_SCALE = float(2**18)


def encode(x):
    x = x * CODE_SCALE
    return (x * x * (x * jnp.abs(x))).astype(BF16)


def decode(code):
    y = code.astype(F32)
    root = lax.rsqrt(lax.rsqrt(jnp.abs(y))) * (1.0 / CODE_SCALE)
    return jnp.where(y < 0, -root, root)


def dot(left, right):
    return jnp.dot(left, right, preferred_element_type=F32)


def dot_last(left, right):
    return lax.dot_general(left, right, (((1,), (1,)), ((), ())), preferred_element_type=F32)


def dot_first(left, right):
    return lax.dot_general(left, right, (((0,), (0,)), ((), ())), preferred_element_type=F32)


def kernel(
    tok_hbm, cot_hbm, wg_hbm, wu_hbm, wd_hbm,
    out_hbm, tgrad_hbm, ggrad_hbm, ugrad_hbm, dgrad_hbm,
    wg, wu, wd, sg, su, sd,
    mine, rows, other, full, acc, send, recv, sendz, recvz,
    hgu, part, parts, small, ggrad, ugrad, dgrad,
    load_sem, mine_sem, wsib_ss, wsib_rs, gat_ss, gat_rs, oth_ss, oth_rs,
    rs_ss, rs_rs, z_ss, z_rs, ag_ss, ag_rs, half_ss, half_rs, o_ss, o_rs, res_sem,
):
    dp, mp = lax.axis_index("dp"), lax.axis_index("mp")
    core, y, zh = dp % 2, (dp // 2) % RING, dp // 16
    rot = mp % RING
    row_core = mp // RING
    sib = (dp + 1 - 2 * core, mp)
    zother = ((1 - zh) * 16 + y * 2 + core, mp)
    factor = 1.0 / math.sqrt(ROWS * N_MP)

    def remote(src, dst, ss, rs, to):
        return pltpu.make_async_remote_copy(
            src_ref=src, dst_ref=dst, send_sem=ss, recv_sem=rs,
            device_id=to, device_id_type=MESH,
        )

    def await_copy(ref, sem):
        pltpu.make_async_copy(ref, ref, sem).wait()

    def along_y(hops):
        return (zh * 16 + ((y + hops + RING) % RING) * 2 + core, mp)

    def local_block(ring_index):
        return (ring_index + 2 * RING + rot) % RING

    def rows16(index):
        return pl.ds(pl.multiple_of(index * ROWS, ROWS), ROWS)

    started = []

    def start(copy):
        copy.start()
        started.append(copy)
        return copy

    own_loads = [
        pltpu.make_async_copy(src, mine.at[i], mine_sem.at[i])
        for i, src in enumerate((tok_hbm, cot_hbm))
    ]
    for copy in own_loads:
        copy.start()
    loads = [
        pltpu.make_async_copy(src, dst, load_sem.at[i])
        for i, (src, dst) in enumerate(((wg_hbm, wg), (wu_hbm, wu), (wd_hbm, wd)))
    ]
    for copy in loads:
        copy.start()

    worker = dp - core + row_core
    at_home = row_core == core
    peers = [zother] + [along_y(hops) for hops in (1, -1, 2, -2)]
    peers += [(worker, (mp + k) % N_MP) for k in range(1, N_MP)]
    idle = dp - core + 1 - row_core
    peers += [(idle, core * RING + (rot + k) % RING) for k in range(1, RING)]
    barrier = pltpu.get_barrier_semaphore()

    def greet(to):
        pl.semaphore_signal(barrier, inc=1, device_id=to, device_id_type=MESH)

    for to in peers:
        greet(to)
    greet(sib)
    away = jnp.where(at_home, 0, 1)
    pl.when(jnp.logical_not(at_home))(lambda: greet((idle, core * RING + rot)))
    pl.semaphore_wait(barrier, len(peers) + 1 + away)

    z_lo, x = mp // 4, mp % 4
    crossings = []
    for i in range(2):
        own_loads[i].wait()
        source, target = mine.at[i], rows.at[core, i, rot]
        arrived = gat_rs.at[i, core, rot]
        for k, z_to in enumerate((3 - z_lo, (z_lo + 2) % 4, z_lo + 1 - 2 * (z_lo % 2), z_lo)):
            for n, x_step in enumerate((2, 1, 3, 0)):
                if k < 3 or x_step:
                    to = (worker, z_to * 4 + (x + x_step) % 4)
                    start(remote(source, target, gat_ss.at[i, 4 * k + n], arrived, to))
        stay = pltpu.make_async_copy(source, target, arrived)
        cross = remote(source, target, gat_ss.at[i, 15], arrived, sib)
        pl.when(at_home)(stay.start)
        pl.when(jnp.logical_not(at_home))(cross.start)
        crossings.append(cross)
    for j, (src, dst) in enumerate(((wg_hbm, sg), (wu_hbm, su), (wd_hbm, sd))):
        start(remote(src, dst, wsib_ss.at[j], wsib_rs.at[j], sib))

    for copy in loads:
        copy.wait()
    for j, dst in enumerate((sg, su, sd)):
        await_copy(dst, wsib_rs.at[j])

    def arrived_rows(i):
        for side in range(2):
            for b in range(RING):
                await_copy(rows.at[side, i, b], gat_rs.at[i, side, b])
        return rows[core, i].reshape(HALF, -1), rows[1 - core, i].reshape(HALF, -1)

    def block_sum(array, hops):
        return acc[array, rows16(local_block(y + hops)), :]

    def send_sums(slot, array, value, hops):
        send[slot, array] = encode(value)
        start(
            remote(
                send.at[slot, array], recv.at[slot, array],
                rs_ss.at[slot, array], rs_rs.at[slot, array], along_y(hops),
            )
        )

    def received(slot, array):
        await_copy(recv.at[slot, array], rs_rs.at[slot, array])
        return decode(recv[slot, array])

    far_side = (-2, 2, 2)

    def send_terms(arrays):
        for array in arrays:
            send_sums(0, array, block_sum(array, 4), far_side[array])
            send_sums(1, array, block_sum(array, 3), 1)
            send_sums(2, array, block_sum(array, -3), -1)
        for array in arrays:
            send_sums(3, array, block_sum(array, 1), 1)
            send_sums(4, array, block_sum(array, -1), -1)

    near, far = arrived_rows(0)
    acc[0] = dot(near, wg[...]) + dot(far, sg[...])
    acc[1] = dot(near, wu[...]) + dot(far, su[...])
    send_terms((0, 1))
    near, far = arrived_rows(1)
    acc[2] = dot_last(near, wd[...]) + dot_last(far, sd[...])
    send_terms((2,))
    for array in range(3):
        for slot, hops in ((1, 2), (2, -2)):
            value = block_sum(array, hops) + received(slot, array)
            if far_side[array] == hops:
                value += received(0, array)
            send_sums(slot + 4, array, value, hops)
    start(remote(rows.at[1 - core], other, oth_ss, oth_rs, sib))
    totals = []
    for array in range(3):
        total = block_sum(array, 0)
        for slot in (3, 4, 5, 6):
            total += received(slot, array)
        sendz[array] = encode(total)
        start(remote(sendz.at[array], recvz.at[array], z_ss.at[array], z_rs.at[array], zother))
        totals.append(total)

    def swapped(array):
        await_copy(recvz.at[array], z_rs.at[array])
        return totals[array] + decode(recvz[array])

    def block_of(hops):
        return core * RING + local_block(y - hops)

    groups = (slice(0, 1), slice(1, 2), slice(2, 3))

    def spread(lane, group, source, hops):
        ref = hgu.at[block_of(source), groups[group]]
        start(remote(ref, ref, ag_ss.at[lane, group], ag_rs.at[lane, group], along_y(hops)))

    def arrive(lane, group, source):
        await_copy(hgu.at[block_of(source), groups[group]], ag_rs.at[lane, group])

    own = block_of(0)
    gate, up = swapped(0), swapped(1)
    sig = jax.nn.sigmoid(gate)
    hgu[own, 0] = (gate * sig * up).astype(BF16)
    for lane, hops in enumerate((2, -2, 1, -1)):
        spread(lane, 0, 0, hops)
    grad_hidden = swapped(2)
    hgu[own, 1] = (grad_hidden * up * sig * (1.0 + gate * (1.0 - sig))).astype(BF16)
    for lane, hops in enumerate((2, -2)):
        spread(lane, 1, 0, hops)
    hgu[own, 2] = (grad_hidden * gate * sig).astype(BF16)
    for lane, hops in enumerate((2, -2)):
        spread(lane, 2, 0, hops)
    for group in (1, 2):
        for lane, hops in ((2, 1), (3, -1)):
            spread(lane, group, 0, hops)
    for group in range(3):
        for lane, hops in ((0, 2), (1, -2)):
            arrive(lane, group, hops)
            spread(lane + 4, group, hops, hops // 2)
            if hops == far_side[group]:
                spread(6, group, hops, hops)
    for group in range(3):
        arrive(2, group, 1)
        arrive(3, group, -1)

    finals = []

    def deliver(which, side, batch, values):
        for n, hops in enumerate(batch):
            slot = (hops + RING) % RING * 2 + side
            index = block_of(hops)
            part[which, slot] = values[n * ROWS : (n + 1) * ROWS].astype(BF16)
            src, dst = part.at[which, slot], parts.at[which, mp]
            sems = o_ss.at[which, slot], o_rs.at[which, mp]
            copy = remote(src, dst, *sems, (sib[0] if side else dp, index))
            if side == 0:
                stay = pltpu.make_async_copy(src, dst, sems[1])
                pl.when(index == mp)(stay.start)
                pl.when(index != mp)(copy.start)
                finals.append((copy, index))
            else:
                start(copy)

    def stacked(array, batch):
        return jnp.concatenate([hgu[block_of(hops), array] for hops in batch], axis=0)

    def multiply_hidden(batch):
        hidden = stacked(0, batch)
        for side, down_w in enumerate((wd, sd)):
            deliver(0, side, batch, dot(hidden, down_w[...]))

    def multiply_grads(batch):
        grad_gate, grad_up = stacked(1, batch), stacked(2, batch)
        for side, (gate_w, up_w) in enumerate(((wg, wu), (sg, su))):
            value = dot_last(grad_gate, gate_w[...]) + dot_last(grad_up, up_w[...])
            deliver(1, side, batch, value)

    def arrive_far(group):
        arrive(4, group, 3)
        arrive(5, group, -3)
        arrive(6, group, 4)

    multiply_hidden((0, 1, -1, 2, -2))
    multiply_grads((0, 1, -1, 2, -2))
    arrive_far(0)
    multiply_hidden((3, -3, 4))
    arrive_far(1)
    arrive_far(2)
    multiply_grads((3, -3, 4))

    my_half = hgu.at[pl.ds(pl.multiple_of(core * RING, RING), RING)]
    their_half = hgu.at[pl.ds(pl.multiple_of((1 - core) * RING, RING), RING)]
    start(remote(my_half, my_half, half_ss, half_rs, sib))
    await_copy(other, oth_rs)
    for i in range(2):
        full[i, pl.ds(pl.multiple_of(core * HALF, HALF), HALF), :] = (
            rows[core, i].reshape(HALF, -1)
        )
        full[i, pl.ds(pl.multiple_of((1 - core) * HALF, HALF), HALF), :] = (
            other[i].reshape(HALF, -1)
        )

    results = []

    def store(src, dst):
        copy = pltpu.make_async_copy(src, dst, res_sem.at[len(results)])
        copy.start()
        results.append(copy)

    await_copy(their_half, half_rs)
    hidden = hgu[:, 0].reshape(2 * HALF, -1)
    grad_gate = hgu[:, 1].reshape(2 * HALF, -1)
    grad_up = hgu[:, 2].reshape(2 * HALF, -1)
    ggrad[...] = (dot_first(full[0], grad_gate) * factor).astype(BF16)
    store(ggrad, ggrad_hbm)
    ugrad[...] = (dot_first(full[0], grad_up) * factor).astype(BF16)
    store(ugrad, ugrad_hbm)
    dgrad[...] = (dot_first(hidden, full[1]) * factor).astype(BF16)
    store(dgrad, dgrad_hbm)

    for which, target in enumerate((out_hbm, tgrad_hbm)):
        total = jnp.zeros((ROWS, 256), F32)
        for k in range(N_MP):
            await_copy(parts.at[which, k], o_rs.at[which, k])
            total += parts[which, k].astype(F32)
        small[which] = total.astype(BF16)
        store(small.at[which], target)

    for copy in started:
        copy.wait_send()
    for cross in crossings:
        pl.when(jnp.logical_not(at_home))(cross.wait_send)
    for copy, index in finals:
        pl.when(index != mp)(copy.wait_send)
    for copy in results:
        copy.wait()


def copy_out(*refs):
    sources, targets, staged, sems = refs[:5], refs[5:10], refs[10:15], refs[15]
    loads = [
        pltpu.make_async_copy(src, mid, sems.at[0, i])
        for i, (src, mid) in enumerate(zip(sources, staged))
    ]
    stores = [
        pltpu.make_async_copy(mid, dst, sems.at[1, i])
        for i, (mid, dst) in enumerate(zip(staged, targets))
    ]
    for copy in loads:
        copy.start()
    for load, store in zip(loads, stores):
        load.wait()
        store.start()
    for copy in stores:
        copy.wait()


def on_device(tokens, gate_weight, up_weight, down_weight, cotangent):
    count, width = tokens.shape
    units = gate_weight.shape[1]
    hbm = pl.BlockSpec(memory_space=pltpu.HBM)
    dma = pltpu.SemaphoreType.DMA

    def vmem(*shape, dtype=BF16):
        return pltpu.VMEM(shape, dtype)

    shapes = (
        jax.ShapeDtypeStruct((count, width), BF16),
        jax.ShapeDtypeStruct((count, width), BF16),
        jax.ShapeDtypeStruct((width, units), BF16),
        jax.ShapeDtypeStruct((width, units), BF16),
        jax.ShapeDtypeStruct((units, width), BF16),
    )
    results = pl.pallas_call(
        kernel,
        out_shape=shapes,
        in_specs=[hbm] * 5,
        out_specs=[hbm] * 5,
        scratch_shapes=[
            vmem(width, units), vmem(width, units), vmem(units, width),
            vmem(width, units), vmem(width, units), vmem(units, width),
            vmem(2, ROWS, width), vmem(2, 2, RING, ROWS, width), vmem(2, RING, ROWS, width),
            vmem(2, 2 * HALF, width), vmem(3, HALF, units, dtype=F32),
            vmem(7, 3, ROWS, units), vmem(7, 3, ROWS, units),
            vmem(3, ROWS, units), vmem(3, ROWS, units),
            vmem(N_MP, 3, ROWS, units),
            vmem(2, N_MP, ROWS, width), vmem(2, N_MP, ROWS, width), vmem(2, ROWS, width),
            vmem(width, units), vmem(width, units), vmem(units, width),
            dma((3,)), dma((2,)), dma((3,)), dma((3,)), dma((2, N_MP)), dma((2, 2, RING)),
            dma(()), dma(()), dma((7, 3)), dma((7, 3)), dma((3,)), dma((3,)),
            dma((7, 3)), dma((7, 3)), dma(()), dma(()), dma((2, N_MP)), dma((2, N_MP)), dma((5,)),
        ],
        compiler_params=pltpu.CompilerParams(
            collective_id=0, has_side_effects=True, vmem_limit_bytes=VMEM_LIMIT
        ),
    )(tokens, cotangent, gate_weight, up_weight, down_weight)
    return pl.pallas_call(
        copy_out,
        out_shape=shapes,
        in_specs=[hbm] * 5,
        out_specs=[hbm] * 5,
        scratch_shapes=[pltpu.VMEM(s.shape, s.dtype) for s in shapes] + [dma((2, 5))],
        compiler_params=pltpu.CompilerParams(vmem_limit_bytes=VMEM_LIMIT),
    )(*results)


def solution(mesh):
    in_specs = (P("mp", "dp"), P("dp", "mp"), P("dp", "mp"), P("mp", "dp"), P("mp", "dp"))
    out_specs = (P("mp", "dp"), P("mp", "dp"), P("dp", "mp"), P("dp", "mp"), P("mp", "dp"))
    return jax.shard_map(
        on_device, mesh=mesh, in_specs=in_specs, out_specs=out_specs, check_vma=False
    )
```

```python
import math

import jax
import jax.numpy as jnp
from jax import lax
from jax.experimental import pallas as pl
from jax.experimental.pallas import tpu as pltpu
from jax.sharding import PartitionSpec as P

MESH = pl.DeviceIdType.MESH
F32 = jnp.float32
BF16 = jnp.bfloat16
RING = 8
ROWS = 16
HALF = RING * ROWS
N_MP = 16
VMEM_LIMIT = 62 * 2**20
CODE_SCALE = float(2**18)


def encode(x):
    x = x * CODE_SCALE
    return (x * x * (x * jnp.abs(x))).astype(BF16)


def decode(code):
    y = code.astype(F32)
    root = lax.rsqrt(lax.rsqrt(jnp.abs(y))) * (1.0 / CODE_SCALE)
    return jnp.where(y < 0, -root, root)


def dot(left, right):
    return jnp.dot(left, right, preferred_element_type=F32)


def dot_last(left, right):
    return lax.dot_general(left, right, (((1,), (1,)), ((), ())), preferred_element_type=F32)


def dot_first(left, right):
    return lax.dot_general(left, right, (((0,), (0,)), ((), ())), preferred_element_type=F32)


def kernel(
    tok_hbm, cot_hbm, wg_hbm, wu_hbm, wd_hbm,
    out_hbm, tgrad_hbm, ggrad_hbm, ugrad_hbm, dgrad_hbm,
    wg, wu, wd, sg, su, sd,
    mine, rows, other, full, acc, send, recv, sendz, recvz,
    hgu, part, parts, small, ggrad, ugrad, dgrad,
    load_sem, mine_sem, wsib_ss, wsib_rs, gat_ss, gat_rs, oth_ss, oth_rs,
    rs_ss, rs_rs, z_ss, z_rs, ag_ss, ag_rs, half_ss, half_rs, o_ss, o_rs, res_sem,
):
    dp, mp = lax.axis_index("dp"), lax.axis_index("mp")
    core, y, zh = dp % 2, (dp // 2) % RING, dp // 16
    rot = mp % RING
    row_core = mp // RING
    sib = (dp + 1 - 2 * core, mp)
    zother = ((1 - zh) * 16 + y * 2 + core, mp)
    factor = 1.0 / math.sqrt(ROWS * N_MP)

    def remote(src, dst, ss, rs, to):
        return pltpu.make_async_remote_copy(
            src_ref=src, dst_ref=dst, send_sem=ss, recv_sem=rs,
            device_id=to, device_id_type=MESH,
        )

    def await_copy(ref, sem):
        pltpu.make_async_copy(ref, ref, sem).wait()

    def along_y(hops):
        return (zh * 16 + ((y + hops + RING) % RING) * 2 + core, mp)

    def local_block(ring_index):
        return (ring_index + 2 * RING + rot) % RING

    def rows16(index):
        return pl.ds(pl.multiple_of(index * ROWS, ROWS), ROWS)

    started = []

    def start(copy):
        copy.start()
        started.append(copy)
        return copy

    own_loads = [
        pltpu.make_async_copy(src, mine.at[i], mine_sem.at[i])
        for i, src in enumerate((tok_hbm, cot_hbm))
    ]
    for copy in own_loads:
        copy.start()
    loads = [
        pltpu.make_async_copy(src, dst, load_sem.at[i])
        for i, (src, dst) in enumerate(((wg_hbm, wg), (wu_hbm, wu), (wd_hbm, wd)))
    ]
    for copy in loads:
        copy.start()

    worker = dp - core + row_core
    at_home = row_core == core
    peers = [zother] + [along_y(hops) for hops in (1, -1, 2, -2)]
    peers += [(worker, (mp + k) % N_MP) for k in range(1, N_MP)]
    idle = dp - core + 1 - row_core
    peers += [(idle, core * RING + (rot + k) % RING) for k in range(1, RING)]
    barrier = pltpu.get_barrier_semaphore()

    def greet(to):
        pl.semaphore_signal(barrier, inc=1, device_id=to, device_id_type=MESH)

    for to in peers:
        greet(to)
    greet(sib)
    away = jnp.where(at_home, 0, 1)
    pl.when(jnp.logical_not(at_home))(lambda: greet((idle, core * RING + rot)))
    pl.semaphore_wait(barrier, len(peers) + 1 + away)

    z_lo, x = mp // 4, mp % 4
    crossings = []
    for i in range(2):
        own_loads[i].wait()
        source, target = mine.at[i], rows.at[core, i, rot]
        arrived = gat_rs.at[i, core, rot]
        for k, z_to in enumerate((3 - z_lo, (z_lo + 2) % 4, z_lo + 1 - 2 * (z_lo % 2), z_lo)):
            for n, x_step in enumerate((2, 1, 3, 0)):
                if k < 3 or x_step:
                    to = (worker, z_to * 4 + (x + x_step) % 4)
                    start(remote(source, target, gat_ss.at[i, 4 * k + n], arrived, to))
        stay = pltpu.make_async_copy(source, target, arrived)
        cross = remote(source, target, gat_ss.at[i, 15], arrived, sib)
        pl.when(at_home)(stay.start)
        pl.when(jnp.logical_not(at_home))(cross.start)
        crossings.append(cross)
        for j in ((0, 1), (2,))[i]:
            src, dst = ((wg_hbm, sg), (wu_hbm, su), (wd_hbm, sd))[j]
            start(remote(src, dst, wsib_ss.at[j], wsib_rs.at[j], sib))


    def arrived_rows(i):
        for side in range(2):
            for b in range(RING):
                await_copy(rows.at[side, i, b], gat_rs.at[i, side, b])
        return rows[core, i].reshape(HALF, -1), rows[1 - core, i].reshape(HALF, -1)

    def block_sum(array, hops):
        return acc[array, rows16(local_block(y + hops)), :]

    def send_sums(slot, array, value, hops):
        send[slot, array] = encode(value)
        start(
            remote(
                send.at[slot, array], recv.at[slot, array],
                rs_ss.at[slot, array], rs_rs.at[slot, array], along_y(hops),
            )
        )

    def received(slot, array):
        await_copy(recv.at[slot, array], rs_rs.at[slot, array])
        return decode(recv[slot, array])

    far_side = (-2, 2, 2)

    def send_terms(array):
        send_sums(0, array, block_sum(array, 4), far_side[array])
        send_sums(1, array, block_sum(array, 3), 1)
        send_sums(2, array, block_sum(array, -3), -1)

    def arrived_weights(j, dst):
        loads[j].wait()
        await_copy(dst, wsib_rs.at[j])

    arrived_weights(0, sg)
    arrived_weights(1, su)
    near, far = arrived_rows(0)
    acc[0] = dot(near, wg[...]) + dot(far, sg[...])
    send_terms(0)
    acc[1] = dot(near, wu[...]) + dot(far, su[...])
    send_terms(1)
    arrived_weights(2, sd)
    near, far = arrived_rows(1)
    acc[2] = dot_last(near, wd[...]) + dot_last(far, sd[...])
    send_terms(2)
    for array in range(3):
        send_sums(3, array, block_sum(array, 1), 1)
        send_sums(4, array, block_sum(array, -1), -1)
    for array in range(3):
        for slot, hops in ((1, 2), (2, -2)):
            value = block_sum(array, hops) + received(slot, array)
            if far_side[array] == hops:
                value += received(0, array)
            send_sums(slot + 4, array, value, hops)
    start(remote(rows.at[1 - core], other, oth_ss, oth_rs, sib))
    totals = []
    for array in range(3):
        total = block_sum(array, 0)
        for slot in (3, 4, 5, 6):
            total += received(slot, array)
        sendz[array] = encode(total)
        start(remote(sendz.at[array], recvz.at[array], z_ss.at[array], z_rs.at[array], zother))
        totals.append(total)

    def swapped(array):
        await_copy(recvz.at[array], z_rs.at[array])
        return totals[array] + decode(recvz[array])

    def block_of(hops):
        return core * RING + local_block(y - hops)

    groups = (slice(0, 1), slice(1, 2), slice(2, 3))

    def spread(lane, group, source, hops):
        ref = hgu.at[block_of(source), groups[group]]
        start(remote(ref, ref, ag_ss.at[lane, group], ag_rs.at[lane, group], along_y(hops)))

    def arrive(lane, group, source):
        await_copy(hgu.at[block_of(source), groups[group]], ag_rs.at[lane, group])

    own = block_of(0)
    gate, up = swapped(0), swapped(1)
    sig = jax.nn.sigmoid(gate)
    hgu[own, 0] = (gate * sig * up).astype(BF16)
    for lane, hops in enumerate((2, -2)):
        spread(lane, 0, 0, hops)
    grad_hidden = swapped(2)
    hgu[own, 1] = (grad_hidden * up * sig * (1.0 + gate * (1.0 - sig))).astype(BF16)
    for lane, hops in enumerate((2, -2)):
        spread(lane, 1, 0, hops)
    hgu[own, 2] = (grad_hidden * gate * sig).astype(BF16)
    for lane, hops in enumerate((2, -2)):
        spread(lane, 2, 0, hops)
    for group in range(3):
        for lane, hops in ((2, 1), (3, -1)):
            spread(lane, group, 0, hops)
    for group in range(3):
        for lane, hops in ((0, 2), (1, -2)):
            arrive(lane, group, hops)
            spread(lane + 4, group, hops, hops // 2)
            if hops == far_side[group]:
                spread(6, group, hops, hops)
    for group in range(3):
        arrive(2, group, 1)
        arrive(3, group, -1)

    finals = []

    def deliver(which, side, batch, values):
        for n, hops in enumerate(batch):
            slot = (hops + RING) % RING * 2 + side
            index = block_of(hops)
            part[which, slot] = values[n * ROWS : (n + 1) * ROWS].astype(BF16)
            src, dst = part.at[which, slot], parts.at[which, mp]
            sems = o_ss.at[which, slot], o_rs.at[which, mp]
            copy = remote(src, dst, *sems, (sib[0] if side else dp, index))
            if side == 0:
                stay = pltpu.make_async_copy(src, dst, sems[1])
                pl.when(index == mp)(stay.start)
                pl.when(index != mp)(copy.start)
                finals.append((copy, index))
            else:
                start(copy)

    def stacked(array, batch):
        return jnp.concatenate([hgu[block_of(hops), array] for hops in batch], axis=0)

    def multiply_hidden(batch):
        hidden = stacked(0, batch)
        for side, down_w in enumerate((wd, sd)):
            deliver(0, side, batch, dot(hidden, down_w[...]))

    def multiply_grads(batch):
        grad_gate, grad_up = stacked(1, batch), stacked(2, batch)
        for side, (gate_w, up_w) in enumerate(((wg, wu), (sg, su))):
            value = dot_last(grad_gate, gate_w[...]) + dot_last(grad_up, up_w[...])
            deliver(1, side, batch, value)

    def arrive_far(group):
        arrive(4, group, 3)
        arrive(5, group, -3)
        arrive(6, group, 4)

    multiply_hidden((0, 1, -1, 2, -2))
    multiply_grads((0, 1, -1, 2, -2))
    arrive_far(0)
    multiply_hidden((3, -3, 4))
    arrive_far(1)
    arrive_far(2)
    multiply_grads((3, -3, 4))

    my_half = hgu.at[pl.ds(pl.multiple_of(core * RING, RING), RING)]
    their_half = hgu.at[pl.ds(pl.multiple_of((1 - core) * RING, RING), RING)]
    start(remote(my_half, my_half, half_ss, half_rs, sib))
    await_copy(other, oth_rs)
    for i in range(2):
        full[i, pl.ds(pl.multiple_of(core * HALF, HALF), HALF), :] = (
            rows[core, i].reshape(HALF, -1)
        )
        full[i, pl.ds(pl.multiple_of((1 - core) * HALF, HALF), HALF), :] = (
            other[i].reshape(HALF, -1)
        )

    results = []

    def store(src, dst):
        copy = pltpu.make_async_copy(src, dst, res_sem.at[len(results)])
        copy.start()
        results.append(copy)

    await_copy(their_half, half_rs)
    hidden = hgu[:, 0].reshape(2 * HALF, -1)
    grad_gate = hgu[:, 1].reshape(2 * HALF, -1)
    grad_up = hgu[:, 2].reshape(2 * HALF, -1)
    ggrad[...] = (dot_first(full[0], grad_gate) * factor).astype(BF16)
    store(ggrad, ggrad_hbm)
    ugrad[...] = (dot_first(full[0], grad_up) * factor).astype(BF16)
    store(ugrad, ugrad_hbm)
    dgrad[...] = (dot_first(hidden, full[1]) * factor).astype(BF16)
    store(dgrad, dgrad_hbm)

    for which, target in enumerate((out_hbm, tgrad_hbm)):
        total = jnp.zeros((ROWS, 256), F32)
        for k in range(N_MP):
            await_copy(parts.at[which, k], o_rs.at[which, k])
            total += parts[which, k].astype(F32)
        small[which] = total.astype(BF16)
        store(small.at[which], target)

    for copy in started:
        copy.wait_send()
    for cross in crossings:
        pl.when(jnp.logical_not(at_home))(cross.wait_send)
    for copy, index in finals:
        pl.when(index != mp)(copy.wait_send)
    for copy in results:
        copy.wait()


def copy_out(*refs):
    sources, targets, staged, sems = refs[:5], refs[5:10], refs[10:15], refs[15]
    loads = [
        pltpu.make_async_copy(src, mid, sems.at[0, i])
        for i, (src, mid) in enumerate(zip(sources, staged))
    ]
    stores = [
        pltpu.make_async_copy(mid, dst, sems.at[1, i])
        for i, (mid, dst) in enumerate(zip(staged, targets))
    ]
    for copy in loads:
        copy.start()
    for load, store in zip(loads, stores):
        load.wait()
        store.start()
    for copy in stores:
        copy.wait()


def on_device(tokens, gate_weight, up_weight, down_weight, cotangent):
    count, width = tokens.shape
    units = gate_weight.shape[1]
    hbm = pl.BlockSpec(memory_space=pltpu.HBM)
    dma = pltpu.SemaphoreType.DMA

    def vmem(*shape, dtype=BF16):
        return pltpu.VMEM(shape, dtype)

    shapes = (
        jax.ShapeDtypeStruct((count, width), BF16),
        jax.ShapeDtypeStruct((count, width), BF16),
        jax.ShapeDtypeStruct((width, units), BF16),
        jax.ShapeDtypeStruct((width, units), BF16),
        jax.ShapeDtypeStruct((units, width), BF16),
    )
    results = pl.pallas_call(
        kernel,
        out_shape=shapes,
        in_specs=[hbm] * 5,
        out_specs=[hbm] * 5,
        scratch_shapes=[
            vmem(width, units), vmem(width, units), vmem(units, width),
            vmem(width, units), vmem(width, units), vmem(units, width),
            vmem(2, ROWS, width), vmem(2, 2, RING, ROWS, width), vmem(2, RING, ROWS, width),
            vmem(2, 2 * HALF, width), vmem(3, HALF, units, dtype=F32),
            vmem(7, 3, ROWS, units), vmem(7, 3, ROWS, units),
            vmem(3, ROWS, units), vmem(3, ROWS, units),
            vmem(N_MP, 3, ROWS, units),
            vmem(2, N_MP, ROWS, width), vmem(2, N_MP, ROWS, width), vmem(2, ROWS, width),
            vmem(width, units), vmem(width, units), vmem(units, width),
            dma((3,)), dma((2,)), dma((3,)), dma((3,)), dma((2, N_MP)), dma((2, 2, RING)),
            dma(()), dma(()), dma((7, 3)), dma((7, 3)), dma((3,)), dma((3,)),
            dma((7, 3)), dma((7, 3)), dma(()), dma(()), dma((2, N_MP)), dma((2, N_MP)), dma((5,)),
        ],
        compiler_params=pltpu.CompilerParams(
            collective_id=0, has_side_effects=True, vmem_limit_bytes=VMEM_LIMIT
        ),
    )(tokens, cotangent, gate_weight, up_weight, down_weight)
    return pl.pallas_call(
        copy_out,
        out_shape=shapes,
        in_specs=[hbm] * 5,
        out_specs=[hbm] * 5,
        scratch_shapes=[pltpu.VMEM(s.shape, s.dtype) for s in shapes] + [dma((2, 5))],
        compiler_params=pltpu.CompilerParams(vmem_limit_bytes=VMEM_LIMIT),
    )(*results)


def solution(mesh):
    in_specs = (P("mp", "dp"), P("dp", "mp"), P("dp", "mp"), P("mp", "dp"), P("mp", "dp"))
    out_specs = (P("mp", "dp"), P("mp", "dp"), P("dp", "mp"), P("dp", "mp"), P("mp", "dp"))
    return jax.shard_map(
        on_device, mesh=mesh, in_specs=in_specs, out_specs=out_specs, check_vma=False
    )
```

```python
import math

import jax
import jax.numpy as jnp
from jax import lax
from jax.experimental import pallas as pl
from jax.experimental.pallas import tpu as pltpu
from jax.sharding import PartitionSpec as P

MESH = pl.DeviceIdType.MESH
F32 = jnp.float32
BF16 = jnp.bfloat16
RING = 8
ROWS = 16
HALF = RING * ROWS
N_MP = 16
VMEM_LIMIT = 62 * 2**20
CODE_SCALE = float(2**18)


def encode(x):
    x = x * CODE_SCALE
    return (x * x * (x * jnp.abs(x))).astype(BF16)


def decode(code):
    y = code.astype(F32)
    root = lax.rsqrt(lax.rsqrt(jnp.abs(y))) * (1.0 / CODE_SCALE)
    return jnp.where(y < 0, -root, root)


def dot(left, right):
    return jnp.dot(left, right, preferred_element_type=F32)


def dot_last(left, right):
    return lax.dot_general(left, right, (((1,), (1,)), ((), ())), preferred_element_type=F32)


def dot_first(left, right):
    return lax.dot_general(left, right, (((0,), (0,)), ((), ())), preferred_element_type=F32)


def kernel(
    tok_hbm, cot_hbm, wg_hbm, wu_hbm, wd_hbm,
    out_hbm, tgrad_hbm, ggrad_hbm, ugrad_hbm, dgrad_hbm,
    wg, wu, wd, sg, su, sd,
    mine, rows, other, full, acc, send, recv, sendz, recvz,
    hgu, part, parts, small, ggrad, ugrad, dgrad,
    load_sem, mine_sem, wsib_ss, wsib_rs, gat_ss, gat_rs, oth_ss, oth_rs,
    rs_ss, rs_rs, z_ss, z_rs, ag_ss, ag_rs, half_ss, half_rs, o_ss, o_rs, res_sem,
):
    dp, mp = lax.axis_index("dp"), lax.axis_index("mp")
    core, y, zh = dp % 2, (dp // 2) % RING, dp // 16
    rot = mp % RING
    row_core = mp // RING
    sib = (dp + 1 - 2 * core, mp)
    zother = ((1 - zh) * 16 + y * 2 + core, mp)
    factor = 1.0 / math.sqrt(ROWS * N_MP)

    def remote(src, dst, ss, rs, to):
        return pltpu.make_async_remote_copy(
            src_ref=src, dst_ref=dst, send_sem=ss, recv_sem=rs,
            device_id=to, device_id_type=MESH,
        )

    def await_copy(ref, sem):
        pltpu.make_async_copy(ref, ref, sem).wait()

    def along_y(hops):
        return (zh * 16 + ((y + hops + RING) % RING) * 2 + core, mp)

    def local_block(ring_index):
        return (ring_index + 2 * RING + rot) % RING

    def rows16(index):
        return pl.ds(pl.multiple_of(index * ROWS, ROWS), ROWS)

    started = []

    def start(copy):
        copy.start()
        started.append(copy)
        return copy

    own_loads = [
        pltpu.make_async_copy(src, mine.at[i], mine_sem.at[i])
        for i, src in enumerate((tok_hbm, cot_hbm))
    ]
    for copy in own_loads:
        copy.start()
    loads = [
        pltpu.make_async_copy(src, dst, load_sem.at[i])
        for i, (src, dst) in enumerate(((wg_hbm, wg), (wu_hbm, wu), (wd_hbm, wd)))
    ]
    for copy in loads:
        copy.start()

    worker = dp - core + row_core
    at_home = row_core == core
    peers = [zother] + [along_y(hops) for hops in (1, -1, 2, -2)]
    peers += [(worker, (mp + k) % N_MP) for k in range(1, N_MP)]
    idle = dp - core + 1 - row_core
    peers += [(idle, core * RING + (rot + k) % RING) for k in range(1, RING)]
    barrier = pltpu.get_barrier_semaphore()

    def greet(to):
        pl.semaphore_signal(barrier, inc=1, device_id=to, device_id_type=MESH)

    for to in peers:
        greet(to)
    greet(sib)
    away = jnp.where(at_home, 0, 1)
    pl.when(jnp.logical_not(at_home))(lambda: greet((idle, core * RING + rot)))
    pl.semaphore_wait(barrier, len(peers) + 1 + away)

    z_lo, x = mp // 4, mp % 4
    crossings = []
    for i in range(2):
        own_loads[i].wait()
        source, target = mine.at[i], rows.at[core, i, rot]
        arrived = gat_rs.at[i, core, rot]
        for k, z_to in enumerate((3 - z_lo, (z_lo + 2) % 4, z_lo + 1 - 2 * (z_lo % 2), z_lo)):
            for n, x_step in enumerate((2, 1, 3, 0)):
                if k < 3 or x_step:
                    to = (worker, z_to * 4 + (x + x_step) % 4)
                    start(remote(source, target, gat_ss.at[i, 4 * k + n], arrived, to))
        stay = pltpu.make_async_copy(source, target, arrived)
        cross = remote(source, target, gat_ss.at[i, 15], arrived, sib)
        pl.when(at_home)(stay.start)
        pl.when(jnp.logical_not(at_home))(cross.start)
        crossings.append(cross)
        for j in ((0, 1), (2,))[i]:
            src, dst = ((wg_hbm, sg), (wu_hbm, su), (wd_hbm, sd))[j]
            start(remote(src, dst, wsib_ss.at[j], wsib_rs.at[j], sib))


    def arrived_rows(i):
        for side in range(2):
            for b in range(RING):
                await_copy(rows.at[side, i, b], gat_rs.at[i, side, b])
        return rows[core, i].reshape(HALF, -1), rows[1 - core, i].reshape(HALF, -1)

    def block_sum(array, hops):
        return acc[array, rows16(local_block(y + hops)), :]

    def send_sums(slot, array, value, hops):
        send[slot, array] = encode(value)
        start(
            remote(
                send.at[slot, array], recv.at[slot, array],
                rs_ss.at[slot, array], rs_rs.at[slot, array], along_y(hops),
            )
        )

    def received(slot, array):
        await_copy(recv.at[slot, array], rs_rs.at[slot, array])
        return decode(recv[slot, array])

    far_side = (-2, 2, 2)

    def send_terms(array):
        send_sums(0, array, block_sum(array, 4), far_side[array])
        send_sums(1, array, block_sum(array, 3), 1)
        send_sums(2, array, block_sum(array, -3), -1)

    def arrived_weights(j, dst):
        loads[j].wait()
        await_copy(dst, wsib_rs.at[j])

    arrived_weights(0, sg)
    arrived_weights(1, su)
    near, far = arrived_rows(0)
    acc[0] = dot(near, wg[...]) + dot(far, sg[...])
    send_terms(0)
    acc[1] = dot(near, wu[...]) + dot(far, su[...])
    send_terms(1)
    arrived_weights(2, sd)
    near, far = arrived_rows(1)
    acc[2] = dot_last(near, wd[...]) + dot_last(far, sd[...])
    send_terms(2)
    for array in range(3):
        send_sums(3, array, block_sum(array, 1), 1)
        send_sums(4, array, block_sum(array, -1), -1)
    for array in range(3):
        for slot, hops in ((1, 2), (2, -2)):
            value = block_sum(array, hops) + received(slot, array)
            if far_side[array] == hops:
                value += received(0, array)
            send_sums(slot + 4, array, value, hops)
    totals = []
    for array in range(3):
        total = block_sum(array, 0)
        for slot in (3, 4, 5, 6):
            total += received(slot, array)
        sendz[array] = encode(total)
        start(remote(sendz.at[array], recvz.at[array], z_ss.at[array], z_rs.at[array], zother))
        totals.append(total)

    def swapped(array):
        await_copy(recvz.at[array], z_rs.at[array])
        return totals[array] + decode(recvz[array])

    def block_of(hops):
        return core * RING + local_block(y - hops)

    groups = (slice(0, 1), slice(1, 2), slice(2, 3))

    def spread(lane, group, source, hops):
        ref = hgu.at[block_of(source), groups[group]]
        start(remote(ref, ref, ag_ss.at[lane, group], ag_rs.at[lane, group], along_y(hops)))

    def arrive(lane, group, source):
        await_copy(hgu.at[block_of(source), groups[group]], ag_rs.at[lane, group])

    own = block_of(0)
    gate, up = swapped(0), swapped(1)
    sig = jax.nn.sigmoid(gate)
    hgu[own, 0] = (gate * sig * up).astype(BF16)
    for lane, hops in enumerate((2, -2)):
        spread(lane, 0, 0, hops)
    grad_hidden = swapped(2)
    hgu[own, 1] = (grad_hidden * up * sig * (1.0 + gate * (1.0 - sig))).astype(BF16)
    for lane, hops in enumerate((2, -2)):
        spread(lane, 1, 0, hops)
    hgu[own, 2] = (grad_hidden * gate * sig).astype(BF16)
    for lane, hops in enumerate((2, -2)):
        spread(lane, 2, 0, hops)
    for group in range(3):
        for lane, hops in ((2, 1), (3, -1)):
            spread(lane, group, 0, hops)
    for group in range(3):
        for lane, hops in ((0, 2), (1, -2)):
            arrive(lane, group, hops)
            spread(lane + 4, group, hops, hops // 2)
            if hops == far_side[group]:
                spread(6, group, hops, hops)
    for group in range(3):
        arrive(2, group, 1)
        arrive(3, group, -1)

    finals = []

    def deliver(which, side, batch, values):
        for n, hops in enumerate(batch):
            slot = (hops + RING) % RING * 2 + side
            index = block_of(hops)
            part[which, slot] = values[n * ROWS : (n + 1) * ROWS].astype(BF16)
            src, dst = part.at[which, slot], parts.at[which, mp]
            sems = o_ss.at[which, slot], o_rs.at[which, mp]
            copy = remote(src, dst, *sems, (sib[0] if side else dp, index))
            if side == 0:
                stay = pltpu.make_async_copy(src, dst, sems[1])
                pl.when(index == mp)(stay.start)
                pl.when(index != mp)(copy.start)
                finals.append((copy, index))
            else:
                start(copy)

    def stacked(array, batch):
        return jnp.concatenate([hgu[block_of(hops), array] for hops in batch], axis=0)

    def multiply_hidden(batch):
        hidden = stacked(0, batch)
        for side, down_w in enumerate((wd, sd)):
            deliver(0, side, batch, dot(hidden, down_w[...]))

    def multiply_grads(batch):
        grad_gate, grad_up = stacked(1, batch), stacked(2, batch)
        for side, (gate_w, up_w) in enumerate(((wg, wu), (sg, su))):
            value = dot_last(grad_gate, gate_w[...]) + dot_last(grad_up, up_w[...])
            deliver(1, side, batch, value)

    def arrive_far(group):
        arrive(4, group, 3)
        arrive(5, group, -3)
        arrive(6, group, 4)

    start(remote(rows.at[1 - core], other, oth_ss, oth_rs, sib))
    multiply_hidden((0, 1, -1, 2, -2))
    multiply_grads((0, 1, -1, 2, -2))
    arrive_far(0)
    multiply_hidden((3, -3, 4))
    arrive_far(1)
    arrive_far(2)
    multiply_grads((3, -3, 4))

    my_half = hgu.at[pl.ds(pl.multiple_of(core * RING, RING), RING)]
    their_half = hgu.at[pl.ds(pl.multiple_of((1 - core) * RING, RING), RING)]
    start(remote(my_half, my_half, half_ss, half_rs, sib))
    await_copy(other, oth_rs)
    for i in range(2):
        full[i, pl.ds(pl.multiple_of(core * HALF, HALF), HALF), :] = (
            rows[core, i].reshape(HALF, -1)
        )
        full[i, pl.ds(pl.multiple_of((1 - core) * HALF, HALF), HALF), :] = (
            other[i].reshape(HALF, -1)
        )

    results = []

    def store(src, dst):
        copy = pltpu.make_async_copy(src, dst, res_sem.at[len(results)])
        copy.start()
        results.append(copy)

    await_copy(their_half, half_rs)
    hidden = hgu[:, 0].reshape(2 * HALF, -1)
    grad_gate = hgu[:, 1].reshape(2 * HALF, -1)
    grad_up = hgu[:, 2].reshape(2 * HALF, -1)
    ggrad[...] = (dot_first(full[0], grad_gate) * factor).astype(BF16)
    store(ggrad, ggrad_hbm)
    ugrad[...] = (dot_first(full[0], grad_up) * factor).astype(BF16)
    store(ugrad, ugrad_hbm)
    dgrad[...] = (dot_first(hidden, full[1]) * factor).astype(BF16)
    store(dgrad, dgrad_hbm)

    for which, target in enumerate((out_hbm, tgrad_hbm)):
        total = jnp.zeros((ROWS, 256), F32)
        for k in range(N_MP):
            await_copy(parts.at[which, k], o_rs.at[which, k])
            total += parts[which, k].astype(F32)
        small[which] = total.astype(BF16)
        store(small.at[which], target)

    for copy in started:
        copy.wait_send()
    for cross in crossings:
        pl.when(jnp.logical_not(at_home))(cross.wait_send)
    for copy, index in finals:
        pl.when(index != mp)(copy.wait_send)
    for copy in results:
        copy.wait()


def copy_out(*refs):
    sources, targets, staged, sems = refs[:5], refs[5:10], refs[10:15], refs[15]
    loads = [
        pltpu.make_async_copy(src, mid, sems.at[0, i])
        for i, (src, mid) in enumerate(zip(sources, staged))
    ]
    stores = [
        pltpu.make_async_copy(mid, dst, sems.at[1, i])
        for i, (mid, dst) in enumerate(zip(staged, targets))
    ]
    for copy in loads:
        copy.start()
    for load, store in zip(loads, stores):
        load.wait()
        store.start()
    for copy in stores:
        copy.wait()


def on_device(tokens, gate_weight, up_weight, down_weight, cotangent):
    count, width = tokens.shape
    units = gate_weight.shape[1]
    hbm = pl.BlockSpec(memory_space=pltpu.HBM)
    dma = pltpu.SemaphoreType.DMA

    def vmem(*shape, dtype=BF16):
        return pltpu.VMEM(shape, dtype)

    shapes = (
        jax.ShapeDtypeStruct((count, width), BF16),
        jax.ShapeDtypeStruct((count, width), BF16),
        jax.ShapeDtypeStruct((width, units), BF16),
        jax.ShapeDtypeStruct((width, units), BF16),
        jax.ShapeDtypeStruct((units, width), BF16),
    )
    results = pl.pallas_call(
        kernel,
        out_shape=shapes,
        in_specs=[hbm] * 5,
        out_specs=[hbm] * 5,
        scratch_shapes=[
            vmem(width, units), vmem(width, units), vmem(units, width),
            vmem(width, units), vmem(width, units), vmem(units, width),
            vmem(2, ROWS, width), vmem(2, 2, RING, ROWS, width), vmem(2, RING, ROWS, width),
            vmem(2, 2 * HALF, width), vmem(3, HALF, units, dtype=F32),
            vmem(7, 3, ROWS, units), vmem(7, 3, ROWS, units),
            vmem(3, ROWS, units), vmem(3, ROWS, units),
            vmem(N_MP, 3, ROWS, units),
            vmem(2, N_MP, ROWS, width), vmem(2, N_MP, ROWS, width), vmem(2, ROWS, width),
            vmem(width, units), vmem(width, units), vmem(units, width),
            dma((3,)), dma((2,)), dma((3,)), dma((3,)), dma((2, N_MP)), dma((2, 2, RING)),
            dma(()), dma(()), dma((7, 3)), dma((7, 3)), dma((3,)), dma((3,)),
            dma((7, 3)), dma((7, 3)), dma(()), dma(()), dma((2, N_MP)), dma((2, N_MP)), dma((5,)),
        ],
        compiler_params=pltpu.CompilerParams(
            collective_id=0, has_side_effects=True, vmem_limit_bytes=VMEM_LIMIT
        ),
    )(tokens, cotangent, gate_weight, up_weight, down_weight)
    return pl.pallas_call(
        copy_out,
        out_shape=shapes,
        in_specs=[hbm] * 5,
        out_specs=[hbm] * 5,
        scratch_shapes=[pltpu.VMEM(s.shape, s.dtype) for s in shapes] + [dma((2, 5))],
        compiler_params=pltpu.CompilerParams(vmem_limit_bytes=VMEM_LIMIT),
    )(*results)


def solution(mesh):
    in_specs = (P("mp", "dp"), P("dp", "mp"), P("dp", "mp"), P("mp", "dp"), P("mp", "dp"))
    out_specs = (P("mp", "dp"), P("mp", "dp"), P("dp", "mp"), P("dp", "mp"), P("mp", "dp"))
    return jax.shard_map(
        on_device, mesh=mesh, in_specs=in_specs, out_specs=out_specs, check_vma=False
    )
```
